256 devices in a mesh: dp: 32 (over y_lo, z, core), feat: 8 (over x, y_hi).
Axes of the slice: x: 4, y: 4 (y_hi: 2, y_lo: 2; y = y_hi * 2 + y_lo), z: 8, core: 2. Of those that a mesh axis runs over, the one named last changes fastest.
Arguments:
- image_feats: bfloat16 [32768, 1664], P(('dp', 'feat')), may hold values from -10 to 10
- text_feats: bfloat16 [32768, 1280], P(('dp', 'feat')), may hold values from -8 to 8
- image_head: bfloat16 [1664, 1280], replicated, may hold values from -0.09928379 to 0.09928379
- text_head: bfloat16 [1280, 1280], replicated, may hold values from -0.11320094 to 0.11320094
- sign_image: int32 [1664, 64], replicated, may hold values from 0 to 1
- sign_embed: int32 [1280, 64], replicated, may hold values from 0 to 1
- test_grads: bfloat16 [512, 4096], P(None, 'feat'), may hold values from -6 to 6
- subset_masks: int32 [256, 32768], P(None, ('dp', 'feat')), may hold values 0 or 1
Outputs:
- subset_scores: float32 [256, 512], P('dp', 'feat')
The draws below stay inside these ranges and needn't reach their ends.
All inputs are finite; a program needn't handle non-finite values. No bound on the sum of `subset_masks` on one device may be relied on, other than what follows from the above.
Results may differ from the reference program's by a relative error of at most 0.0035.
The reference program's roundings to bfloat16 on the way count: a program that leaves them out, or rounds other values in their place, can miss the bound.
Values may be sent and summed in bfloat16 or wider, within the bound.
A program may use at most 128 MiB of HBM per device.

```python
import math
import jax
import jax.numpy as jnp
from jax import lax

VW = 1664
TW = 1280
E = 1280
K1 = 64
K2 = 64
TESTS = 512
SUBSETS = 256
PROJ = 4096
PAIRS = 32768


def mixed_normal(key, shape):
    normal_part = jnp.clip(jax.random.normal(jax.random.fold_in(key, 1), shape, jnp.float32), -6.0, 6.0)
    return normal_part


def pair_plan(key, lowest, highest):
    index = jnp.arange(PAIRS)
    even_rows = index % 2 == 0
    picked = jax.random.uniform(jax.random.fold_in(key, 21), (PAIRS,), jnp.float32) < 0.25
    leader = jnp.logical_and(even_rows, picked)
    partner = jnp.roll(leader, 1)
    spread = jax.random.uniform(jax.random.fold_in(key, 22), (PAIRS,), jnp.float32)
    level = lowest + (highest - lowest) * jnp.sqrt(spread)
    level = jnp.where(partner, 0.985 * jnp.roll(level, 1), level)
    base = mixed_normal(jax.random.fold_in(key, 23), (PAIRS, TW))
    mixed_text = 0.97 * jnp.roll(base, 1, axis=0) + math.sqrt(1.0 - 0.97 * 0.97) * base
    text = jnp.where(partner[:, None], mixed_text, base)
    matched = jnp.logical_or(leader, partner)
    return (matched, level, text)


def head_shared(key):
    return jnp.clip(jax.random.normal(jax.random.fold_in(key, 31), (TW, E), jnp.float32), -4.0, 4.0)


def draw_text_feats(key, part):
    matched, level, text = pair_plan(key, 0.3, 0.97)
    return jnp.clip(text, -8.0, 8.0).astype(jnp.bfloat16)


def draw_image_feats(key, part):
    matched, level, text = pair_plan(key, 0.3, 0.97)
    key = jax.random.fold_in(key, 5)
    first_noise = mixed_normal(jax.random.fold_in(key, 1), (PAIRS, TW))
    tail_noise = mixed_normal(jax.random.fold_in(key, 2), (PAIRS, VW - TW))
    ratio = 1.0 / (level * level) - 1.0
    near = jnp.sqrt(0.5 * ratio)
    far = jnp.sqrt(0.5 * ratio * TW / (VW - TW))
    first = jnp.where(matched[:, None], text + near[:, None] * first_noise, first_noise)
    tail = jnp.where(matched[:, None], far[:, None] * tail_noise, tail_noise)
    joined = jnp.concatenate([first, tail], axis=1)
    return jnp.clip(joined, -10.0, 10.0).astype(jnp.bfloat16)


def draw_text_head(key, part):
    shared = head_shared(key)
    return (shared / math.sqrt(TW)).astype(jnp.bfloat16)


def draw_image_head(key, part):
    shared = head_shared(key)
    key = jax.random.fold_in(key, 9)
    tail = jnp.clip(jax.random.normal(key, (VW - TW, E), jnp.float32), -4.0, 4.0)
    joined = jnp.concatenate([shared, tail], axis=0) / math.sqrt(VW)
    return joined.astype(jnp.bfloat16)


def place_ends(entries, key, low, largest):
    shape = entries.shape
    spot = [jax.random.randint(jax.random.fold_in(key, axis), (), 0, shape[axis]) for axis in range(len(shape))]
    entries = entries.at[tuple(spot)].set(low)
    longest = shape.index(max(shape))
    spot[longest] = (spot[longest] + 1) % shape[longest]
    return entries.at[tuple(spot)].set(largest)


def level_of(stream_key, dims, split, least, largest):
    def one(axis_at, blocks):
        draws = jax.random.uniform(jax.random.fold_in(jax.random.fold_in(stream_key, 6), axis_at), (blocks,), jnp.float32, least / len(split), largest / len(split))
        return jnp.repeat(jnp.exp(draws), dims[axis_at] // blocks).reshape((-1,) + (1,) * (len(dims) - axis_at - 1))

    loudness = one(*split[0])
    for cut in split[1:]:
        loudness = loudness * one(*cut)
    return loudness


def bell_draw(rng, shape, scale, reach, pieces=(), held_as=jnp.bfloat16):
    array = jax.random.normal(rng, shape, jnp.float32) * scale
    if len(pieces) > 0:
        array = level_of(rng, shape, pieces, -0.22, 0.18) * array
    return jnp.clip(array, min=-reach, max=reach).astype(held_as)


def setup_inputs(seed: int = 0) -> dict:
    key_list = jax.random.split(jax.random.key(seed), 9)
    return {
        "image_feats": draw_image_feats(jax.random.fold_in(key_list[8], 71), 0),
        "text_feats": draw_text_feats(jax.random.fold_in(key_list[8], 71), 0),
        "image_head": draw_image_head(jax.random.fold_in(key_list[8], 71), 0),
        "text_head": draw_text_head(jax.random.fold_in(key_list[8], 71), 0),
        "sign_image": place_ends(jax.random.randint(key_list[4], (VW, K1), 0, 2), jax.random.fold_in(key_list[4], 1), 0, 1).astype(jnp.int32),
        "sign_embed": place_ends(jax.random.randint(key_list[5], (E, K2), 0, 2), jax.random.fold_in(key_list[5], 1), 0, 1).astype(jnp.int32),
        "test_grads": bell_draw(key_list[6], (TESTS, PROJ), 1.0, 6.0, ((1, 8),)),
        "subset_masks": place_ends((jax.random.randint(key_list[7], (SUBSETS, PAIRS), 0, 2) < 1).astype(jnp.int32), jax.random.fold_in(key_list[7], 1), 0, 1),
    }


def normalized(feats, head):
    proj = jnp.dot(feats, head, preferred_element_type=jnp.float32)
    length = jnp.sqrt(lax.optimization_barrier(jnp.sum(proj * proj, axis=1)) + 1e-06)
    return ((proj / length[:, None]).astype(jnp.bfloat16), length)

def reference(image_feats, text_feats, image_head, text_head, sign_image, sign_embed, test_grads, subset_masks):
    z_image, norm_image = normalized(image_feats, image_head)
    z_text, _ = normalized(text_feats, text_head)
    signs_embed = (2 * sign_embed - 1).astype(jnp.bfloat16)
    signs_image = (2 * sign_image - 1).astype(jnp.bfloat16)
    zr_text = jnp.dot(z_text, signs_embed, preferred_element_type=jnp.float32).astype(jnp.bfloat16)
    zr_image = jnp.dot(z_image, signs_embed, preferred_element_type=jnp.float32)
    block_rows = min(512, PAIRS)
    blocks = z_image.reshape(PAIRS // block_rows, block_rows, E)

    def first_pass(carry, block):
        col_max, col_sum = carry
        logits = 100.0 * jnp.dot(block, z_text.T, preferred_element_type=jnp.float32)
        row_max = lax.optimization_barrier(jnp.max(logits, axis=1))
        row_lse = row_max + jnp.log(lax.optimization_barrier(jnp.sum(jnp.exp(logits - row_max[:, None]), axis=1)))
        new_max = jnp.maximum(col_max, lax.optimization_barrier(jnp.max(logits, axis=0)))
        new_sum = col_sum * jnp.exp(col_max - new_max) + lax.optimization_barrier(jnp.sum(jnp.exp(logits - new_max[None, :]), axis=0))
        return ((new_max, new_sum), row_lse)
    start = (jnp.full((PAIRS,), -1e+30, jnp.float32), jnp.zeros((PAIRS,), jnp.float32))
    (col_max, col_sum), row_lse = lax.scan(first_pass, start, blocks)
    col_lse = col_max + jnp.log(col_sum)
    row_lse = row_lse.reshape(PAIRS // block_rows, block_rows)

    def second_pass(items):
        block, lse_block = items
        logits = 100.0 * jnp.dot(block, z_text.T, preferred_element_type=jnp.float32)
        weights = (jnp.exp(logits - lse_block[:, None]) + jnp.exp(logits - col_lse[None, :])).astype(jnp.bfloat16)
        pulled = 50.0 * jnp.dot(weights, zr_text, preferred_element_type=jnp.float32)
        radial = 0.5 * lax.optimization_barrier(jnp.sum(weights.astype(jnp.float32) * logits, axis=1))
        return (pulled, radial)
    pulled, radial = lax.map(second_pass, (blocks, row_lse))
    pulled = pulled.reshape(PAIRS, K2) - 100.0 * zr_text.astype(jnp.float32)
    own_logit = 100.0 * lax.optimization_barrier(jnp.sum(z_image.astype(jnp.float32) * z_text.astype(jnp.float32), axis=1))
    radial = radial.reshape(PAIRS) - own_logit
    grad_proj = (pulled - radial[:, None] * zr_image) / norm_image[:, None]
    feat_proj = jnp.dot(image_feats, signs_image, preferred_element_type=jnp.float32)
    phi = (feat_proj[:, :, None] * grad_proj[:, None, :]).reshape(PAIRS, PROJ) / jnp.sqrt(jnp.float32(VW))
    phi = phi.astype(jnp.bfloat16)
    scores = jnp.dot(phi, test_grads.T, preferred_element_type=jnp.float32)
    total = jnp.dot(subset_masks.astype(jnp.float32), scores, precision=lax.Precision.HIGHEST)
    return total / jnp.sqrt(jnp.float32(PAIRS * PROJ))
```

```python
import functools
import math

import jax
import jax.numpy as jnp
from jax import lax
from jax.experimental import pallas as pl
from jax.experimental.pallas import tpu as pltpu
from jax.sharding import PartitionSpec as P

X, Y = 4, 4
LANES = 128
LOG2E = math.log2(math.e)
MESH = pl.DeviceIdType.MESH
NT = (((1,), (1,)), ((), ()))


def dot_nt(a, b):
    return lax.dot_general(a, b, NT, preferred_element_type=jnp.float32)


def lse2(parts):
    top = functools.reduce(jnp.maximum, parts)
    total = functools.reduce(lambda a, b: a + b, [jnp.exp2(p - top) for p in parts])
    return top + jnp.log2(total)


class Names:
    def __init__(self):
        self.ids = {}

    def __call__(self, name):
        return self.ids.setdefault(name, len(self.ids))


def kernel(
    cfg,
    zi_ref, zt_ref, feats_ref, sgne_ref, sgni_ref, norm_ref, mask_ref, tg_hbm,
    out_ref,
    img, txt, logit, zr, tmax, tsum, imax, isum, rbuf, cbuf, msg, precv, fbuf, gall, frecv,
    maskall, phi, tg, tot, crecv, pk, prs, acc2, zrs, send_sem, recv_sem, tg_sem,
):
    pairs, Z, TB = cfg["pairs"], cfg["Z"], cfg["TB"]
    IB = Y * pairs
    n_text = 2 * Z * pairs
    half, quarter = pairs // 2, pairs // 4
    dp, feat = lax.axis_index("dp"), lax.axis_index("feat")
    c = dp % 2
    z = (dp // 2) % Z
    yl = dp // (2 * Z)
    x = feat // 2
    y = (feat % 2) * 2 + yl

    def dev(dx=0, dy=0, dz=0, dc=0):
        xx, yy, zz, cc = (x + dx) % X, (y + dy) % Y, (z + dz) % Z, (c + dc) % 2
        return {"dp": ((yy % 2) * Z + zz) * 2 + cc, "feat": xx * 2 + yy // 2}

    plane = [(dx, dy) for dx in range(X) for dy in range(Y) if (dx, dy) != (0, 0)]
    line = [(dz, dc) for dc in range(2) for dz in range(Z) if (dz, dc) != (0, 0)]

    barrier = pltpu.get_barrier_semaphore()
    for dx, dy in plane:
        pl.semaphore_signal(barrier, inc=1, device_id=dev(dx, dy), device_id_type=MESH)
    for dz, dc in line:
        pl.semaphore_signal(barrier, inc=1, device_id=dev(0, 0, dz, dc), device_id_type=MESH)
    pl.semaphore_wait(barrier, len(plane) + len(line))

    names = Names()
    started = []

    def send(name, src, dst, to):
        i = names(name)
        copy = pltpu.make_async_remote_copy(
            src_ref=src, dst_ref=dst, send_sem=send_sem.at[i], recv_sem=recv_sem.at[i],
            device_id=to, device_id_type=MESH,
        )
        copy.start()
        started.append(copy)

    def recv(name, dst):
        i = names(name)
        pltpu.make_async_remote_copy(
            src_ref=dst, dst_ref=dst, send_sem=send_sem.at[i], recv_sem=recv_sem.at[i],
            device_id=dev(1), device_id_type=MESH,
        ).wait_recv()

    def drain():
        for copy in started:
            copy.wait_send()
        started.clear()

    def image(dx, dy, r0, n):
        return img.at[pl.ds((((x + dx) % X) * Y + (y + dy) % Y) * pairs + r0, n), :]

    def text(dz, dc, r0, n):
        return txt.at[pl.ds((((c + dc) % 2) * Z + (z + dz) % Z) * pairs + r0, n), :]

    tg_copy = pltpu.make_async_copy(tg_hbm, tg, tg_sem)
    tg_copy.start()

    own_slot = x * Y + y
    img[pl.ds(own_slot * pairs, pairs), :] = zi_ref[...]
    txt[pl.ds((c * Z + z) * pairs, pairs), :] = zt_ref[...]

    HZ = Z // 2

    def span(s, up):
        if s < HZ - 1:
            return 0, pairs
        return (0, half) if up else (half, half)

    def text_send(s):
        for up, step in ((True, 1), (False, -1)):
            r0, n = span(s, up)
            block = text(-s * step, 0, r0, n)
            send(f"z{step}{s}", block, block, dev(0, 0, step, 0))

    def text_recv(s):
        for up, step in ((True, 1), (False, -1)):
            r0, n = span(s, up)
            recv(f"z{step}{s}", text(-(s + 1) * step, 0, r0, n))
        far = (HZ,) if s == HZ - 1 else (-(s + 1), s + 1)
        for dz in far:
            block = text(dz, 0, 0, pairs)
            send(f"s{dz}", block, block, dev(0, 0, 0, 1))

    def plane_dirs(which):
        return ((1, 0), (0, 1)) if which == 0 else ((0, 1), (1, 0))

    def at(which, a, b, r0, n):
        (fx, fy), (gx, gy) = plane_dirs(which)
        return image(fx * a + gx * b, fy * a + gy * b, which * half + r0, n)

    def first_send(which):
        (fx, fy), _ = plane_dirs(which)
        block = at(which, 0, 0, 0, half)
        for d in (1, -1):
            send(f"f{which}{d}", block, block, dev(fx * d, fy * d))

    def first_forward(which):
        (fx, fy), _ = plane_dirs(which)
        for d in (1, -1):
            recv(f"f{which}{d}", at(which, -d, 0, 0, half))
            block = at(which, -d, 0, 0 if d == 1 else quarter, quarter)
            send(f"F{which}{d}", block, block, dev(fx * d, fy * d))

    def first_last(which):
        for d in (1, -1):
            recv(f"F{which}{d}", at(which, 2, 0, 0 if d == 1 else quarter, quarter))

    def second_send(which, a):
        _, (gx, gy) = plane_dirs(which)
        block = at(which, a, 0, 0, half)
        for d in (1, -1):
            send(f"g{which}{a}{d}", block, block, dev(gx * d, gy * d))

    def second_forward(which, a):
        _, (gx, gy) = plane_dirs(which)
        for d in (1, -1):
            recv(f"g{which}{a}{d}", at(which, a, -d, 0, half))
            block = at(which, a, -d, 0 if d == 1 else quarter, quarter)
            send(f"G{which}{a}{d}", block, block, dev(gx * d, gy * d))

    def second_last(which, a):
        for d in (1, -1):
            recv(f"G{which}{a}{d}", at(which, a, 2, 0 if d == 1 else quarter, quarter))

    text_send(0)
    for which in (0, 1):
        first_send(which)
    for which in (0, 1):
        second_send(which, 0)
    block = text(0, 0, 0, pairs)
    send("s0", block, block, dev(0, 0, 0, 1))

    own_image, own_text = zi_ref[...], zt_ref[...]
    izr = dot_nt(sgne_ref[...], own_image)
    own_zr = dot_nt(sgne_ref[...], own_text).astype(jnp.bfloat16).astype(jnp.float32)
    prod = own_image.astype(jnp.float32) * own_text.astype(jnp.float32)
    width = prod.shape[1]
    lanes = functools.reduce(
        lambda a, b: a + b, [prod[:, k : k + LANES] for k in range(0, width, LANES)]
    )
    own_logit = 100.0 * jnp.sum(lanes.T, axis=0, keepdims=True)
    fbuf[...] = dot_nt(sgni_ref[...], feats_ref[...])
    tmax[...] = jnp.full(tmax.shape, -1e30, jnp.float32)
    tsum[...] = jnp.zeros(tsum.shape, jnp.float32)
    imax[...] = jnp.full(imax.shape, -1e30, jnp.float32)
    isum[...] = jnp.zeros(isum.shape, jnp.float32)

    for which in (0, 1):
        first_forward(which)
        second_send(which, -1)
        second_send(which, 1)
    for s in range(1, HZ):
        text_recv(s - 1)
        text_send(s)
        if s == 1:
            for which in (0, 1):
                second_forward(which, 0)
            for which in (0, 1):
                first_last(which)
                second_send(which, 2)
        if s == 2:
            for which in (0, 1):
                for a in (-1, 1):
                    second_forward(which, a)
    text_recv(HZ - 1)
    if HZ < 2:
        for which in (0, 1):
            second_forward(which, 0)
        for which in (0, 1):
            first_last(which)
            second_send(which, 2)
    if HZ < 3:
        for which in (0, 1):
            for a in (-1, 1):
                second_forward(which, a)
    for which in (0, 1):
        second_forward(which, 2)
    for which in (0, 1):
        for a in (0, -1, 1, 2):
            second_last(which, a)
    for dz in range(-(HZ - 1), HZ + 1):
        recv(f"s{dz}", text(dz, 1, 0, pairs))

    for xx in range(X):
        for yy in range(2):
            if (xx, yy) == (0, 0):
                continue
            to = dev(xx, 2 * yy)
            send(f"m{xx}{yy}", mask_ref, maskall.at[:, pl.ds(feat * pairs, pairs)], to)
            src = fbuf.at[pl.ds(to["feat"] * 8, 8), :]
            send(f"r{xx}{yy}", src, frecv.at[feat], to)
    maskall[:, pl.ds(pl.multiple_of(feat * pairs, pairs), pairs)] = mask_ref[...]
    frecv[feat] = fbuf[pl.ds(pl.multiple_of(feat * 8, 8), 8), :]

    scale = 100.0 * LOG2E

    def first_pass(step, carry):
        ic, tj = step // (n_text // TB), step % (n_text // TB)
        rows = pl.ds(pl.multiple_of(tj * TB, TB), TB)
        block = dot_nt(txt[rows, :], img[pl.ds(pl.multiple_of(ic * IB, IB), IB), :]) * scale
        logit[ic, rows, :] = block
        deep = block.reshape(TB // 8, 8, IB)
        old = imax[ic]
        new = jnp.maximum(old, jnp.max(deep, axis=0))
        isum[ic] = isum[ic] * jnp.exp2(old - new) + jnp.sum(jnp.exp2(deep - new[None]), axis=0)
        imax[ic] = new
        parts = [block[:, k : k + LANES] for k in range(0, IB, LANES)]
        old = tmax[rows, :]
        new = functools.reduce(jnp.maximum, parts, old)
        tsum[rows, :] = functools.reduce(
            lambda a, b: a + b,
            [jnp.exp2(p - new) for p in parts],
            tsum[rows, :] * jnp.exp2(old - new),
        )
        tmax[rows, :] = new
        return carry

    lax.fori_loop(0, X * (n_text // TB), first_pass, 0)

    for ic in range(X):
        top = jnp.max(imax[ic], axis=0, keepdims=True)
        total = jnp.sum(isum[ic] * jnp.exp2(imax[ic] - top), axis=0, keepdims=True)
        rbuf[0, ic : ic + 1, :] = top + jnp.log2(total)
    for b in range(n_text // LANES):
        rows = slice(b * LANES, (b + 1) * LANES)
        high = tmax[rows, :].T
        top = jnp.max(high, axis=0, keepdims=True)
        total = jnp.sum(tsum[rows, :].T * jnp.exp2(high - top), axis=0, keepdims=True)
        cbuf[0, b : b + 1, :] = top + jnp.log2(total)

    for k, (dx, dy) in enumerate(plane):
        send(f"R{k}", rbuf.at[0], rbuf.at[k + 1], dev(dx, dy))
    for k, (dz, dc) in enumerate(line):
        send(f"C{k}", cbuf.at[0], cbuf.at[k + 1], dev(0, 0, dz, dc))

    def zr_block(tj, carry):
        rows = pl.ds(pl.multiple_of(tj * TB, TB), TB)
        zr[tj] = dot_nt(sgne_ref[...], txt[rows, :]).astype(jnp.bfloat16)
        return carry

    lax.fori_loop(0, n_text // TB, zr_block, 0)
    drain()

    for k in range(len(plane)):
        recv(f"R{k}", rbuf.at[k + 1])
    for k in range(len(line)):
        recv(f"C{k}", cbuf.at[k + 1])
    row_lse = lse2([rbuf[k] for k in range(len(plane) + 1)])
    rbuf[0] = row_lse
    col_lse = lse2([cbuf[k] for k in range(len(line) + 1)])
    for b in range(n_text // LANES):
        tmax[b * LANES : (b + 1) * LANES, :] = jnp.broadcast_to(
            col_lse[b : b + 1, :], (LANES, LANES)
        ).T

    for dx in (2, 1, 3, 0):
        ic = (x + dx) % X
        row = rbuf[0, pl.ds(ic, 1), :]

        def second_pass(tj, carry):
            acc, radial = carry
            rows = pl.ds(pl.multiple_of(tj * TB, TB), TB)
            block = logit[ic, rows, :]
            col = tmax[rows, :]
            col = jnp.concatenate([col] * (IB // LANES), axis=1)
            weights = (jnp.exp2(block - row) + jnp.exp2(block - col)).astype(jnp.bfloat16)
            acc += jnp.dot(zr[tj], weights, preferred_element_type=jnp.float32)
            radial += jnp.sum(
                (weights.astype(jnp.float32) * block).reshape(TB // 8, 8, IB), axis=0
            )
            return acc, radial

        acc, radial = lax.fori_loop(
            0, n_text // TB, second_pass,
            (jnp.zeros((64, IB), jnp.float32), jnp.zeros((8, IB), jnp.float32)),
        )
        for yy in range(Y):
            cols = slice(yy * pairs, (yy + 1) * pairs)
            msg[ic * Y + yy, 0:64, :] = acc[:, cols]
            msg[ic * Y + yy, 64:72, :] = radial[:, cols]
        for k, (px, py) in enumerate(plane):
            if px == dx:
                send(f"P{k}", msg.at[ic * Y + (y + py) % Y], precv.at[k], dev(px, py))

    total = msg[own_slot]
    for k in range(len(plane)):
        recv(f"P{k}", precv.at[k])
        total += precv[k]
    pulled = 50.0 * total[0:64] - 100.0 * own_zr
    radial = (0.5 / LOG2E) * jnp.sum(total[64:72], axis=0, keepdims=True) - own_logit
    grad = (pulled - radial * izr) / norm_ref[...]
    gall[feat] = grad

    for xx in range(X):
        for yy in range(2):
            if (xx, yy) != (0, 0):
                send(f"g{xx}{yy}", gall.at[feat], gall.at[feat], dev(xx, 2 * yy))
    for xx in range(X):
        for yy in range(2):
            if (xx, yy) != (0, 0):
                came = ((x - xx) % X) * 2 + (feat + yy) % 2
                recv(f"m{xx}{yy}", maskall.at[:, pl.ds(came * pairs, pairs)])
                recv(f"r{xx}{yy}", frecv.at[came])
    tg_copy.wait()
    for xx in range(X):
        for yy in range(2):
            if (xx, yy) != (0, 0):
                came = ((x - xx) % X) * 2 + (feat + yy) % 2
                recv(f"g{xx}{yy}", gall.at[came])

    shrink = 1.0 / math.sqrt(cfg["vw"])
    for f in range(2 * X):
        g = gall[f]
        for a in range(8):
            phi[a * 64 : (a + 1) * 64, f * pairs : (f + 1) * pairs] = (
                frecv[f, a : a + 1, :] * g * shrink
            ).astype(jnp.bfloat16)
    summed = dot_nt(maskall[...], phi[...])
    high = summed.astype(jnp.bfloat16)
    rest = summed - high.astype(jnp.float32)
    mid = rest.astype(jnp.bfloat16)
    low = (rest - mid.astype(jnp.float32)).astype(jnp.bfloat16)
    tests = tg[...]
    scores = dot_nt(high, tests) + (dot_nt(mid, tests) + dot_nt(low, tests))
    tot[...] = scores.reshape(tot.shape)

    send("core", tot.at[:, :, 1 - c], crecv, dev(0, 0, 0, 1))
    recv("core", crecv)
    both = tot[:, :, c] + crecv[...]
    lane = lax.broadcasted_iota(jnp.int32, (HZ * 8, LANES), 1)
    for ylow in range(2):
        low_z = both[ylow, :HZ].reshape(HZ * 8, -1)
        high_z = both[ylow, HZ:].reshape(HZ * 8, -1)
        for xx in range(X):
            cols = slice(xx * LANES, (xx + 1) * LANES)
            a, b = low_z[:, cols], high_z[:, cols]
            first = jnp.where(lane < 64, a, pltpu.roll(b, 64, 1))
            second = jnp.where(lane < 64, pltpu.roll(a, 64, 1), b)
            pk[xx * Y + ylow] = first.reshape(HZ, 8, LANES)
            pk[xx * Y + 2 + ylow] = second.reshape(HZ, 8, LANES)
    for k, (dx, dy) in enumerate(plane):
        send(f"Q{k}", pk.at[((x + dx) % X) * Y + (y + dy) % Y], prs.at[k], dev(dx, dy))
    total = pk[own_slot]
    for k in range(len(plane)):
        recv(f"Q{k}", prs.at[k])
        total += prs[k]
    acc2[...] = total
    for dz in range(1, Z):
        send(f"Z{dz}", acc2.at[(z + dz) % HZ], zrs.at[dz - 1], dev(0, 0, dz, 0))
    total = acc2[z % HZ]
    for dz in range(1, Z):
        recv(f"Z{dz}", zrs.at[dz - 1])
        total += zrs[dz - 1]
    total = jnp.where(z >= HZ, pltpu.roll(total, 64, 1), total)
    out_ref[...] = total[:, :64] * (1.0 / cfg["divide"])
    drain()


def fused(cfg, zi, zt, feats, sgne, sgni, norm, masks, tests):
    pairs, Z, TB = cfg["pairs"], cfg["Z"], cfg["TB"]
    width = zi.shape[1]
    n_image, n_text = X * Y * pairs, 2 * Z * pairs
    subsets, n_tests = masks.shape[0], tests.shape[0]
    f32, bf16 = jnp.float32, jnp.bfloat16
    vmem = pltpu.VMEM
    n_copies = 40 + 2 * Z + 15 + 2 * Z - 1 + 15 + 21 + 1 + 15 + Z - 1
    scratch = [
        vmem((n_image, width), bf16),
        vmem((n_text, width), bf16),
        vmem((X, n_text, Y * pairs), f32),
        vmem((n_text // TB, 64, TB), bf16),
        vmem((n_text, LANES), f32),
        vmem((n_text, LANES), f32),
        vmem((X, 8, Y * pairs), f32),
        vmem((X, 8, Y * pairs), f32),
        vmem((X * Y, X, Y * pairs), f32),
        vmem((2 * Z, n_text // LANES, LANES), f32),
        vmem((X * Y, 72, pairs), f32),
        vmem((X * Y - 1, 72, pairs), f32),
        vmem((64, pairs), f32),
        vmem((2 * X, 64, pairs), f32),
        vmem((2 * X, 8, pairs), f32),
        vmem((subsets, 2 * X * pairs), bf16),
        vmem((512, 2 * X * pairs), bf16),
        vmem(tests.shape, bf16),
        vmem((2, Z, 2, 8, n_tests), f32),
        vmem((2, Z, 8, n_tests), f32),
        vmem((X * Y, Z // 2, 8, LANES), f32),
        vmem((X * Y - 1, Z // 2, 8, LANES), f32),
        vmem((Z // 2, 8, LANES), f32),
        vmem((Z - 1, 8, LANES), f32),
        pltpu.SemaphoreType.DMA((n_copies,)),
        pltpu.SemaphoreType.DMA((n_copies,)),
        pltpu.SemaphoreType.DMA,
    ]
    whole = pl.BlockSpec(memory_space=pltpu.VMEM)
    return pl.pallas_call(
        functools.partial(kernel, cfg),
        out_shape=jax.ShapeDtypeStruct((8, 64), f32),
        in_specs=[whole] * 7 + [pl.BlockSpec(memory_space=pl.ANY)],
        out_specs=whole,
        scratch_shapes=scratch,
        compiler_params=pltpu.CompilerParams(
            collective_id=0, has_side_effects=True, vmem_limit_bytes=60 * 1024 * 1024
        ),
    )(zi, zt, feats, sgne, sgni, norm, masks, tests)


def normalized(feats, head):
    proj = jnp.dot(feats, head, preferred_element_type=jnp.float32)
    length = jnp.sqrt(jnp.sum(proj * proj, axis=1) + 1e-06)
    return (proj / length[:, None]).astype(jnp.bfloat16), length


def on_device(
    image_feats, text_feats, image_head, text_head, sign_image, sign_embed, test_grads, subset_masks
):
    own_text, _ = normalized(text_feats, text_head)
    own_image, norm = normalized(image_feats, image_head)
    pairs = image_feats.shape[0]
    n_devices = lax.axis_size("dp") * lax.axis_size("feat")
    cfg = {
        "pairs": pairs,
        "Z": lax.axis_size("dp") // 4,
        "TB": 256,
        "vw": image_feats.shape[1],
        "divide": math.sqrt(pairs * n_devices * 4096),
    }
    return fused(
        cfg,
        own_image,
        own_text,
        image_feats,
        (2 * sign_embed.T - 1).astype(jnp.bfloat16),
        (2 * sign_image.T - 1).astype(jnp.bfloat16),
        norm[None, :],
        subset_masks.astype(jnp.bfloat16),
        test_grads,
    )


def solution(mesh):
    placed = (
        P(("dp", "feat"), None),
        P(("dp", "feat"), None),
        P(),
        P(),
        P(),
        P(),
        P(None, "feat"),
        P(None, ("dp", "feat")),
    )
    return jax.shard_map(
        on_device, mesh=mesh, in_specs=placed, out_specs=P("dp", "feat"), check_vma=False
    )
```

```python
import functools
import math

import jax
import jax.numpy as jnp
from jax import lax
from jax.experimental import pallas as pl
from jax.experimental.pallas import tpu as pltpu
from jax.sharding import PartitionSpec as P

X, Y = 4, 4
LANES = 128
LOG2E = math.log2(math.e)
MESH = pl.DeviceIdType.MESH
NT = (((1,), (1,)), ((), ()))


def dot_nt(a, b):
    return lax.dot_general(a, b, NT, preferred_element_type=jnp.float32)


def lse2(parts):
    top = functools.reduce(jnp.maximum, parts)
    total = functools.reduce(lambda a, b: a + b, [jnp.exp2(p - top) for p in parts])
    return top + jnp.log2(total)


class Names:
    def __init__(self):
        self.ids = {}

    def __call__(self, name):
        return self.ids.setdefault(name, len(self.ids))


PLANE = (
    (0, 0), (1, 0), (-1, 0), (0, 1),
    (0, -1), (1, 1), (1, -1), (-1, 1),
    (-1, -1), (2, 0), (0, 2), (2, 1),
    (2, -1), (1, 2), (-1, 2), (2, 2),
)


def kernel(
    cfg,
    feats_hbm, tfeats_hbm, ihead_hbm, thead_hbm, signi_hbm, signe_hbm, mask_hbm, tg_hbm,
    out_ref,
    feats, tfeats, ihead, thead, signi, signe, masks, tg,
    sgne, img, txt, logit, zr, tmax, tsum, imax, isum, rbuf, cbuf, rows_lse, msg, precv,
    fbuf, gall, frecv, maskall, phi, tot, crecv, pk, prs, acc2, zrs,
    send_sem, recv_sem, load_sem,
):
    pairs, Z, TB = cfg["pairs"], cfg["Z"], 2 * cfg["pairs"]
    IB = 4 * pairs
    half, quarter = pairs // 2, pairs // 4
    HZ = Z // 2
    order = [0] + [d for k in range(1, HZ) for d in (k, -k)] + [HZ]
    dp, feat = lax.axis_index("dp"), lax.axis_index("feat")
    c = dp & 1
    z = (dp >> 1) & (Z - 1)
    yl = dp >> (Z.bit_length())
    x = feat >> 1
    y = ((feat & 1) << 1) + yl

    xs = [(x + d) & (X - 1) for d in range(X)]
    ys = [(y + d) & (Y - 1) for d in range(Y)]
    zs = [(z + d) & (Z - 1) for d in range(Z)]
    cs = [c, 1 - c]
    x_part = [v << 1 for v in xs]
    y_feat = [v >> 1 for v in ys]
    y_dp = [(v & 1) << (Z.bit_length()) for v in ys]
    z_part = [v << 1 for v in zs]

    def dev(dx=0, dy=0, dz=0, dc=0):
        return {
            "dp": y_dp[dy % Y] + z_part[dz % Z] + cs[dc % 2],
            "feat": x_part[dx % X] + y_feat[dy % Y],
        }

    def image_slot(dx, dy):
        return (xs[dx % X] << 2) + ys[dy % Y]

    def text_slot(dz, dc):
        return cs[dc % 2] * Z + zs[dz % Z]

    plane = PLANE[1:]
    line = [(dz, dc) for dc in range(2) for dz in range(Z) if (dz, dc) != (0, 0)]
    mates = [(dx, 2 * h) for dx in range(X) for h in range(2) if (dx, h) != (0, 0)]

    loads = [
        pltpu.make_async_copy(src, dst, load_sem.at[i])
        for i, (src, dst) in enumerate(
            (
                (tfeats_hbm, tfeats), (thead_hbm, thead), (feats_hbm, feats),
                (ihead_hbm, ihead), (signe_hbm, signe), (signi_hbm, signi),
                (mask_hbm, masks), (tg_hbm, tg),
            )
        )
    ]
    for load in loads:
        load.start()

    barrier = pltpu.get_barrier_semaphore()
    for dx, dy in plane:
        pl.semaphore_signal(barrier, inc=1, device_id=dev(dx, dy), device_id_type=MESH)
    for dz, dc in line:
        pl.semaphore_signal(barrier, inc=1, device_id=dev(0, 0, dz, dc), device_id_type=MESH)

    names = Names()
    started = []

    def send(name, src, dst, to):
        i = names(name)
        copy = pltpu.make_async_remote_copy(
            src_ref=src, dst_ref=dst, send_sem=send_sem.at[i], recv_sem=recv_sem.at[i],
            device_id=to, device_id_type=MESH,
        )
        copy.start()
        started.append(copy)

    def recv(name, dst):
        i = names(name)
        pltpu.make_async_remote_copy(
            src_ref=dst, dst_ref=dst, send_sem=send_sem.at[i], recv_sem=recv_sem.at[i],
            device_id=dev(1), device_id_type=MESH,
        ).wait_recv()

    def drain():
        for copy in started:
            copy.wait_send()
        started.clear()

    def wrap(d, n):
        return (d + n // 2 - 1) % n - (n // 2 - 1)

    def image(dx, dy, r0, n):
        k = PLANE.index((wrap(dx, X), wrap(dy, Y)))
        return img.at[pl.ds(k * pairs + r0, n), :]

    def text(dz, dc, r0, n):
        k = order.index(wrap(dz, Z)) * 2 + dc % 2
        return txt.at[pl.ds(k * pairs + r0, n), :]

    def project(feats_ref, head_ref):
        proj = jnp.dot(feats_ref[...], head_ref[...], preferred_element_type=jnp.float32)
        length = jnp.sqrt(jnp.sum(proj * proj, axis=1, keepdims=True) + 1e-06)
        return (proj / length).astype(jnp.bfloat16), length

    def text_pieces(s, up):
        if s < HZ - 1:
            return (0, 1)
        return (0,) if up else (1,)

    def text_send(s, h):
        for up, step in ((True, 1), (False, -1)):
            if h in text_pieces(s, up):
                src = text(-s * step, 0, h * half, half)
                dst = text(-(s + 1) * step, 0, h * half, half)
                send(f"z{step}{s}{h}", src, dst, dev(0, 0, step, 0))

    def text_recv(s, h):
        for up, step in ((True, 1), (False, -1)):
            if h in text_pieces(s, up):
                recv(f"z{step}{s}{h}", text(-(s + 1) * step, 0, h * half, half))

    def text_share(dz):
        send(f"s{dz}", text(dz, 0, 0, pairs), text(dz, 1, 0, pairs), dev(0, 0, 0, 1))

    def text_shared(dz):
        recv(f"s{dz}", text(dz, 1, 0, pairs))

    def axes(which):
        return ((1, 0), (0, 1)) if which == 0 else ((0, 1), (1, 0))

    def at(which, a, b, r0, n):
        (fx, fy), (gx, gy) = axes(which)
        return image(fx * a + gx * b, fy * a + gy * b, which * half + r0, n)

    def part(d):
        return 0 if d == 1 else quarter

    def first_send(which):
        (fx, fy), _ = axes(which)
        for d in (1, -1):
            src, dst = at(which, 0, 0, 0, half), at(which, -d, 0, 0, half)
            send(f"f{which}{d}", src, dst, dev(fx * d, fy * d))

    def first_forward(which):
        (fx, fy), _ = axes(which)
        for d in (1, -1):
            recv(f"f{which}{d}", at(which, -d, 0, 0, half))
            src = at(which, -d, 0, part(d), quarter)
            send(f"F{which}{d}", src, at(which, 2, 0, part(d), quarter), dev(fx * d, fy * d))

    def first_last(which):
        for d in (1, -1):
            recv(f"F{which}{d}", at(which, 2, 0, part(d), quarter))

    def second_send(which, a):
        _, (gx, gy) = axes(which)
        for d in (1, -1):
            src, dst = at(which, a, 0, 0, half), at(which, a, -d, 0, half)
            send(f"g{which}{a}{d}", src, dst, dev(gx * d, gy * d))

    def second_forward(which, a):
        _, (gx, gy) = axes(which)
        for d in (1, -1):
            recv(f"g{which}{a}{d}", at(which, a, -d, 0, half))
            src = at(which, a, -d, part(d), quarter)
            send(f"G{which}{a}{d}", src, at(which, a, 2, part(d), quarter), dev(gx * d, gy * d))

    def second_last(which, a):
        for d in (1, -1):
            recv(f"G{which}{a}{d}", at(which, a, 2, part(d), quarter))

    scale = 100.0 * LOG2E

    def tile(t, ic):
        rows = pl.ds(t * TB if isinstance(t, int) else pl.multiple_of(t * TB, TB), TB)
        cols = pl.ds(ic * IB if isinstance(ic, int) else pl.multiple_of(ic * IB, IB), IB)
        block = dot_nt(txt[rows, :], img[cols, :]) * scale
        logit[ic, rows, :] = block
        deep = block.reshape(TB // 8, 8, IB)
        old = imax[ic]
        new = jnp.maximum(old, jnp.max(deep, axis=0))
        isum[ic] = isum[ic] * jnp.exp2(old - new) + jnp.sum(jnp.exp2(deep - new[None]), axis=0)
        imax[ic] = new
        parts = [block[:, k : k + LANES] for k in range(0, IB, LANES)]
        old = tmax[rows, :]
        new = functools.reduce(jnp.maximum, parts, old)
        tsum[rows, :] = functools.reduce(
            lambda a, b: a + b,
            [jnp.exp2(p - new) for p in parts],
            tsum[rows, :] * jnp.exp2(old - new),
        )
        tmax[rows, :] = new

    def tiles(n, at_step):
        def body(i, carry):
            for t, ic in at_step(i):
                tile(t, ic)
            return carry

        lax.fori_loop(0, n, body, 0)

    n_t = len(order)

    loads[0].wait()
    loads[1].wait()
    own_text, _ = project(tfeats, thead)
    txt[0:pairs, :] = own_text
    pl.semaphore_wait(barrier, len(plane) + len(line))
    text_send(0, 0)
    text_send(0, 1)
    text_share(0)
    loads[2].wait()
    loads[3].wait()
    own_image, length = project(feats, ihead)
    img[0:pairs, :] = own_image
    for which in (0, 1):
        first_send(which)
    for which in (0, 1):
        second_send(which, 0)

    for i in (4, 5, 6, 7):
        loads[i].wait()
    sgne[...] = (2 * signe[...] - 1).astype(jnp.bfloat16)
    norm = jnp.broadcast_to(length, (pairs, LANES)).T[0:1, :]
    izr = dot_nt(sgne[...], own_image)
    own_zr = dot_nt(sgne[...], own_text).astype(jnp.bfloat16).astype(jnp.float32)
    prod = own_image.astype(jnp.float32) * own_text.astype(jnp.float32)
    lanes = functools.reduce(
        lambda a, b: a + b, [prod[:, k : k + LANES] for k in range(0, prod.shape[1], LANES)]
    )
    own_logit = 100.0 * jnp.sum(lanes.T, axis=0, keepdims=True)
    fbuf[...] = dot_nt((2 * signi[...] - 1).astype(jnp.bfloat16), feats[...])
    mine = pl.ds(pl.multiple_of(feat * pairs, pairs), pairs)
    maskall[:, mine] = masks[...].astype(jnp.bfloat16)
    frecv[feat] = fbuf[pl.ds(pl.multiple_of(feat * 8, 8), 8), :]
    tmax[...] = jnp.full(tmax.shape, -1e30, jnp.float32)
    tsum[...] = jnp.zeros(tsum.shape, jnp.float32)
    imax[...] = jnp.full(imax.shape, -1e30, jnp.float32)
    isum[...] = jnp.zeros(isum.shape, jnp.float32)

    for which in (0, 1):
        first_forward(which)
        second_send(which, -1)
        second_send(which, 1)
    for h in (0, 1):
        text_recv(0, h)
        text_send(1, h)
    text_share(1)
    text_share(-1)
    for which in (0, 1):
        second_forward(which, 0)
    for which in (0, 1):
        first_last(which)
        second_send(which, 2)
    for dz in (0, 1, -1):
        text_shared(dz)
    tiles(3, lambda i: [(i, 0)])
    for h in (0, 1):
        text_recv(1, h)
        text_send(2, h)
    text_share(2)
    text_share(-2)
    for which in (0, 1):
        for a in (-1, 1):
            second_forward(which, a)
    text_shared(2)
    text_shared(-2)
    tiles(2, lambda i: [(i + 3, 0), (i + 3, 1)])
    text_recv(2, 0)
    text_send(3, 0)
    tiles(3, lambda i: [(i, 1)])
    text_recv(2, 1)
    text_send(3, 1)
    text_share(3)
    text_share(-3)
    for which in (0, 1):
        second_forward(which, 2)
    text_shared(3)
    text_shared(-3)
    tiles(2, lambda i: [(i + 5, 0), (i + 5, 1)])
    for which in (0, 1):
        for a in (0, 1):
            second_last(which, a)
    tiles(n_t - 1, lambda i: [(i, 2)])
    text_recv(3, 0)
    text_recv(3, 1)
    text_share(HZ)
    for which in (0, 1):
        for a in (-1, 2):
            second_last(which, a)
    tiles((n_t - 2) // 2, lambda i: [(2 * i, 3), (2 * i + 1, 3)])
    text_shared(HZ)
    tiles(1, lambda i: [(n_t - 2, 3), (n_t - 1, 0), (n_t - 1, 1), (n_t - 1, 2), (n_t - 1, 3)])

    for dx, dy in mates:
        to = dev(dx, dy)
        send(f"m{dx}{dy}", maskall.at[:, mine], maskall.at[:, mine], to)
        send(f"r{dx}{dy}", fbuf.at[pl.ds(to["feat"] * 8, 8), :], frecv.at[feat], to)

    for k, (dx, dy) in enumerate(PLANE):
        ic, cols = k // 4, slice(k % 4 * LANES, (k % 4 + 1) * LANES)
        high = imax[ic, :, cols]
        top = jnp.max(high, axis=0, keepdims=True)
        total = jnp.sum(isum[ic, :, cols] * jnp.exp2(high - top), axis=0, keepdims=True)
        rbuf[0, pl.ds(image_slot(dx, dy), 1), :] = top + jnp.log2(total)
    for k, (dx, dy) in enumerate(plane):
        send(f"R{k}", rbuf.at[0], rbuf.at[k + 1], dev(dx, dy))
    texts = [(dz, dc) for dz in order for dc in range(2)]
    for b, (dz, dc) in enumerate(texts):
        rows = slice(b * LANES, (b + 1) * LANES)
        high = tmax[rows, :].T
        top = jnp.max(high, axis=0, keepdims=True)
        total = jnp.sum(tsum[rows, :].T * jnp.exp2(high - top), axis=0, keepdims=True)
        cbuf[0, pl.ds(text_slot(dz, dc), 1), :] = top + jnp.log2(total)
    for k, (dz, dc) in enumerate(line):
        send(f"C{k}", cbuf.at[0], cbuf.at[k + 1], dev(0, 0, dz, dc))

    for t in range(n_t // 2):
        rows = slice(t * 2 * TB, (t + 1) * 2 * TB)
        zr[t] = dot_nt(sgne[...], txt[rows, :]).astype(jnp.bfloat16)
    drain()

    for k in range(len(plane)):
        recv(f"R{k}", rbuf.at[k + 1])
    rbuf[0] = lse2([rbuf[k] for k in range(len(plane) + 1)])
    for k, (dx, dy) in enumerate(PLANE):
        cols = slice(k % 4 * LANES, (k % 4 + 1) * LANES)
        rows_lse[k // 4, :, cols] = rbuf[0, pl.ds(image_slot(dx, dy), 1), :]
    for k in range(len(line)):
        recv(f"C{k}", cbuf.at[k + 1])
    cbuf[0] = lse2([cbuf[k] for k in range(len(line) + 1)])
    for b, (dz, dc) in enumerate(texts):
        col = cbuf[0, pl.ds(text_slot(dz, dc), 1), :]
        tmax[b * LANES : (b + 1) * LANES, :] = jnp.broadcast_to(col, (LANES, LANES)).T

    for ic in (3, 2, 1, 0):
        row = rows_lse[ic]

        def second_pass(t, carry):
            acc, radial = carry
            rows = pl.ds(pl.multiple_of(t * 2 * TB, 2 * TB), 2 * TB)
            block = logit[ic, rows, :]
            col = tmax[rows, :]
            col = jnp.concatenate([col] * (IB // LANES), axis=1)
            weights = (jnp.exp2(block - row) + jnp.exp2(block - col)).astype(jnp.bfloat16)
            acc += jnp.dot(zr[t], weights, preferred_element_type=jnp.float32)
            radial += jnp.sum(
                (weights.astype(jnp.float32) * block).reshape(2 * TB // 8, 8, IB), axis=0
            )
            return acc, radial

        acc, radial = lax.fori_loop(
            0, n_t // 2, second_pass,
            (jnp.zeros((64, IB), jnp.float32), jnp.zeros((8, IB), jnp.float32)),
        )
        for q in range(4):
            k, cols = ic * 4 + q, slice(q * LANES, (q + 1) * LANES)
            msg[k, 0:64, :] = acc[:, cols]
            msg[k, 64:72, :] = radial[:, cols]
            if k > 0:
                send(f"P{k}", msg.at[k], precv.at[k - 1], dev(*PLANE[k]))

    total = msg[0]
    for k in range(len(PLANE) - 1, 0, -1):
        recv(f"P{k}", precv.at[k - 1])
        total += precv[k - 1]
    pulled = 50.0 * total[0:64] - 100.0 * own_zr
    radial = (0.5 / LOG2E) * jnp.sum(total[64:72], axis=0, keepdims=True) - own_logit
    gall[feat] = (pulled - radial * izr) / norm

    for dx, dy in mates:
        send(f"g{dx}{dy}", gall.at[feat], gall.at[feat], dev(dx, dy))

    def mate(dx, dy):
        return x_part[-dx % X] + y_feat[-dy % Y]

    for dx, dy in mates:
        came = mate(dx, dy)
        recv(f"m{dx}{dy}", maskall.at[:, pl.ds(pl.multiple_of(came * pairs, pairs), pairs)])
        recv(f"r{dx}{dy}", frecv.at[came])
    for dx, dy in mates:
        recv(f"g{dx}{dy}", gall.at[mate(dx, dy)])

    shrink = 1.0 / math.sqrt(cfg["vw"])
    for f in range(2 * X):
        g = gall[f]
        for a in range(8):
            phi[a * 64 : (a + 1) * 64, f * pairs : (f + 1) * pairs] = (
                frecv[f, a : a + 1, :] * g * shrink
            ).astype(jnp.bfloat16)
    summed = dot_nt(maskall[...], phi[...])
    high = summed.astype(jnp.bfloat16)
    rest = summed - high.astype(jnp.float32)
    mid = rest.astype(jnp.bfloat16)
    low = (rest - mid.astype(jnp.float32)).astype(jnp.bfloat16)
    tests = tg[...]
    scores = dot_nt(high, tests) + (dot_nt(mid, tests) + dot_nt(low, tests))
    tot[...] = scores.reshape(tot.shape)

    send("core", tot.at[:, :, 1 - c], crecv, dev(0, 0, 0, 1))
    recv("core", crecv)
    both = tot[:, :, c] + crecv[...]
    lane = lax.broadcasted_iota(jnp.int32, (HZ * 8, LANES), 1)
    for ylow in range(2):
        low_z = both[ylow, :HZ].reshape(HZ * 8, -1)
        high_z = both[ylow, HZ:].reshape(HZ * 8, -1)
        for xx in range(X):
            cols = slice(xx * LANES, (xx + 1) * LANES)
            a, b = low_z[:, cols], high_z[:, cols]
            first = jnp.where(lane < 64, a, pltpu.roll(b, 64, 1))
            second = jnp.where(lane < 64, pltpu.roll(a, 64, 1), b)
            pk[xx * Y + ylow] = first.reshape(HZ, 8, LANES)
            pk[xx * Y + 2 + ylow] = second.reshape(HZ, 8, LANES)
    for k, (dx, dy) in enumerate(plane):
        send(f"Q{k}", pk.at[image_slot(dx, dy)], prs.at[k], dev(dx, dy))
    total = pk[image_slot(0, 0)]
    for k in range(len(plane)):
        recv(f"Q{k}", prs.at[k])
        total += prs[k]
    acc2[...] = total
    for dz in range(1, Z):
        send(f"Z{dz}", acc2.at[zs[dz] & (HZ - 1)], zrs.at[dz - 1], dev(0, 0, dz, 0))
    total = acc2[z & (HZ - 1)]
    for dz in range(1, Z):
        recv(f"Z{dz}", zrs.at[dz - 1])
        total += zrs[dz - 1]
    total = jnp.where(z >= HZ, pltpu.roll(total, 64, 1), total)
    out_ref[...] = total[:, :64] * (1.0 / cfg["divide"])
    drain()


def on_device(*args):
    image_feats, text_feats, image_head, text_head, sign_image, sign_embed, tests, masks = args
    pairs, vw = image_feats.shape
    width = image_head.shape[1]
    Z = lax.axis_size("dp") // 4
    n_devices = lax.axis_size("dp") * lax.axis_size("feat")
    cfg = {"pairs": pairs, "Z": Z, "vw": vw, "divide": math.sqrt(pairs * n_devices * 4096)}
    n_image, n_text = X * Y * pairs, 2 * Z * pairs
    subsets, n_tests = masks.shape[0], tests.shape[0]
    f32, bf16 = jnp.float32, jnp.bfloat16
    vmem = pltpu.VMEM
    operands = (
        image_feats, text_feats, image_head, text_head, sign_image.T, sign_embed.T, masks, tests,
    )
    n_copies = 40 + 4 * Z - 2 + Z + 15 + 2 * Z - 1 + 15 + 21 + 1 + 15 + Z - 1
    scratch = [vmem(value.shape, value.dtype) for value in operands] + [
        vmem((64, width), bf16),
        vmem((n_image, width), bf16),
        vmem((n_text, width), bf16),
        vmem((X * Y // 4, n_text, 4 * pairs), f32),
        vmem((n_text // (4 * pairs), 64, 4 * pairs), bf16),
        vmem((n_text, LANES), f32),
        vmem((n_text, LANES), f32),
        vmem((X * Y // 4, 8, 4 * pairs), f32),
        vmem((X * Y // 4, 8, 4 * pairs), f32),
        vmem((X * Y, X * Y, pairs), f32),
        vmem((2 * Z, 2 * Z, pairs), f32),
        vmem((X * Y // 4, 1, 4 * pairs), f32),
        vmem((X * Y, 72, pairs), f32),
        vmem((X * Y - 1, 72, pairs), f32),
        vmem((64, pairs), f32),
        vmem((2 * X, 64, pairs), f32),
        vmem((2 * X, 8, pairs), f32),
        vmem((subsets, 2 * X * pairs), bf16),
        vmem((512, 2 * X * pairs), bf16),
        vmem((2, Z, 2, 8, n_tests), f32),
        vmem((2, Z, 8, n_tests), f32),
        vmem((X * Y, Z // 2, 8, LANES), f32),
        vmem((X * Y - 1, Z // 2, 8, LANES), f32),
        vmem((Z // 2, 8, LANES), f32),
        vmem((Z - 1, 8, LANES), f32),
        pltpu.SemaphoreType.DMA((n_copies,)),
        pltpu.SemaphoreType.DMA((n_copies,)),
        pltpu.SemaphoreType.DMA((len(operands),)),
    ]
    return pl.pallas_call(
        functools.partial(kernel, cfg),
        out_shape=jax.ShapeDtypeStruct((8, 64), f32),
        in_specs=[pl.BlockSpec(memory_space=pl.ANY)] * len(operands),
        out_specs=pl.BlockSpec(memory_space=pltpu.VMEM),
        scratch_shapes=scratch,
        compiler_params=pltpu.CompilerParams(
            collective_id=0, has_side_effects=True, vmem_limit_bytes=60 * 1024 * 1024
        ),
    )(*operands)


def solution(mesh):
    placed = (
        P(("dp", "feat"), None),
        P(("dp", "feat"), None),
        P(),
        P(),
        P(),
        P(),
        P(None, "feat"),
        P(None, ("dp", "feat")),
    )
    return jax.shard_map(
        on_device, mesh=mesh, in_specs=placed, out_specs=P("dp", "feat"), check_vma=False
    )
```

```python
import functools
import math

import jax
import jax.numpy as jnp
from jax import lax
from jax.experimental import pallas as pl
from jax.experimental.pallas import tpu as pltpu
from jax.sharding import PartitionSpec as P

X, Y = 4, 4
LANES = 128
LOG2E = math.log2(math.e)
MESH = pl.DeviceIdType.MESH
NT = (((1,), (1,)), ((), ()))


def dot_nt(a, b):
    return lax.dot_general(a, b, NT, preferred_element_type=jnp.float32)


def lse2(parts):
    top = functools.reduce(jnp.maximum, parts)
    total = functools.reduce(lambda a, b: a + b, [jnp.exp2(p - top) for p in parts])
    return top + jnp.log2(total)


class Names:
    def __init__(self):
        self.ids = {}

    def __call__(self, name):
        return self.ids.setdefault(name, len(self.ids))


PLANE = (
    (0, 0), (1, 0), (-1, 0), (0, 1),
    (0, -1), (1, 1), (1, -1), (-1, 1),
    (-1, -1), (2, 0), (0, 2), (2, 1),
    (2, -1), (1, 2), (-1, 2), (2, 2),
)


def kernel(
    cfg,
    feats_hbm, tfeats_hbm, ihead_hbm, thead_hbm, signi_hbm, signe_hbm, mask_hbm, tg_hbm,
    out_ref,
    feats, tfeats, ihead, thead, signi, signe, masks, tg,
    sgne, img, txt, logit, zr, tmax, tsum, imax, isum, rbuf, cbuf, rows_lse, msg, precv,
    fbuf, gall, frecv, maskall, phi, tot, crecv, pk, prs, acc2, zrs,
    send_sem, recv_sem, load_sem,
):
    pairs, Z, TB = cfg["pairs"], cfg["Z"], 2 * cfg["pairs"]
    IB = 4 * pairs
    half, quarter = pairs // 2, pairs // 4
    HZ = Z // 2
    order = [0] + [d for k in range(1, HZ) for d in (k, -k)] + [HZ]
    dp, feat = lax.axis_index("dp"), lax.axis_index("feat")
    c = dp & 1
    z = (dp >> 1) & (Z - 1)
    yl = dp >> (Z.bit_length())
    x = feat >> 1
    y = ((feat & 1) << 1) + yl

    xs = [(x + d) & (X - 1) for d in range(X)]
    ys = [(y + d) & (Y - 1) for d in range(Y)]
    zs = [(z + d) & (Z - 1) for d in range(Z)]
    cs = [c, 1 - c]
    x_part = [v << 1 for v in xs]
    y_feat = [v >> 1 for v in ys]
    y_dp = [(v & 1) << (Z.bit_length()) for v in ys]
    z_part = [v << 1 for v in zs]

    def dev(dx=0, dy=0, dz=0, dc=0):
        return {
            "dp": y_dp[dy % Y] + z_part[dz % Z] + cs[dc % 2],
            "feat": x_part[dx % X] + y_feat[dy % Y],
        }

    def image_slot(dx, dy):
        return (xs[dx % X] << 2) + ys[dy % Y]

    def text_slot(dz, dc):
        return cs[dc % 2] * Z + zs[dz % Z]

    plane = PLANE[:0:-1]
    line = order[:0:-1]
    mates = [(2, 1), (1, 1), (-1, 1), (2, 0), (0, 1), (1, 0), (-1, 0)]

    def mate(dx, h):
        return {
            "dp": ((yl ^ h) << Z.bit_length()) + z_part[0] + c,
            "feat": x_part[dx % X] + (y_feat[0] ^ h),
        }

    loads = [
        pltpu.make_async_copy(src, dst, load_sem.at[i])
        for i, (src, dst) in enumerate(
            (
                (feats_hbm, feats), (ihead_hbm, ihead), (tfeats_hbm, tfeats),
                (thead_hbm, thead), (signe_hbm, signe), (signi_hbm, signi),
                (mask_hbm, masks), (tg_hbm, tg),
            )
        )
    ]
    for load in loads:
        load.start()

    barrier = pltpu.get_barrier_semaphore()
    near = [(0, 0, 0, 1)]
    for d in (1, -1):
        near += [(d, 0, 0, 0), (0, d, 0, 0), (0, 0, d, 0)]
    for offsets in near:
        pl.semaphore_signal(barrier, inc=1, device_id=dev(*offsets), device_id_type=MESH)

    names = Names()
    started = []

    def send(name, src, dst, to):
        i = names(name)
        copy = pltpu.make_async_remote_copy(
            src_ref=src, dst_ref=dst, send_sem=send_sem.at[i], recv_sem=recv_sem.at[i],
            device_id=to, device_id_type=MESH,
        )
        copy.start()
        started.append(copy)

    def recv(name, dst):
        i = names(name)
        pltpu.make_async_remote_copy(
            src_ref=dst, dst_ref=dst, send_sem=send_sem.at[i], recv_sem=recv_sem.at[i],
            device_id=dev(1), device_id_type=MESH,
        ).wait_recv()

    def drain():
        for copy in started:
            copy.wait_send()
        started.clear()

    def wrap(d, n):
        return (d + n // 2 - 1) % n - (n // 2 - 1)

    def image(dx, dy, r0, n):
        k = PLANE.index((wrap(dx, X), wrap(dy, Y)))
        return img.at[pl.ds(k * pairs + r0, n), :]

    def text(dz, dc, r0, n):
        k = order.index(wrap(dz, Z)) * 2 + dc % 2
        return txt.at[pl.ds(k * pairs + r0, n), :]

    def project(feats_ref, head_ref):
        proj = jnp.dot(feats_ref[...], head_ref[...], preferred_element_type=jnp.float32)
        length = jnp.sqrt(jnp.sum(proj * proj, axis=1, keepdims=True) + 1e-06)
        return (proj / length).astype(jnp.bfloat16), length

    def text_pieces(s, up):
        if s < HZ - 1:
            return (0, 1)
        return (0,) if up else (1,)

    def text_send(s, h):
        for up, step in ((True, 1), (False, -1)):
            if h in text_pieces(s, up):
                src = text(-s * step, 0, h * half, half)
                dst = text(-(s + 1) * step, 0, h * half, half)
                send(f"z{step}{s}{h}", src, dst, dev(0, 0, step, 0))

    def text_recv(s, h):
        for up, step in ((True, 1), (False, -1)):
            if h in text_pieces(s, up):
                recv(f"z{step}{s}{h}", text(-(s + 1) * step, 0, h * half, half))

    def text_share(dz):
        send(f"s{dz}", text(dz, 0, 0, pairs), text(dz, 1, 0, pairs), dev(0, 0, 0, 1))

    def text_shared(dz):
        recv(f"s{dz}", text(dz, 1, 0, pairs))

    def axes(which):
        return ((1, 0), (0, 1)) if which == 0 else ((0, 1), (1, 0))

    def at(which, a, b, r0, n):
        (fx, fy), (gx, gy) = axes(which)
        return image(fx * a + gx * b, fy * a + gy * b, which * half + r0, n)

    def part(d):
        return 0 if d == 1 else quarter

    def first_send(which):
        (fx, fy), _ = axes(which)
        for d in (1, -1):
            src, dst = at(which, 0, 0, 0, half), at(which, -d, 0, 0, half)
            send(f"f{which}{d}", src, dst, dev(fx * d, fy * d))

    def first_forward(which):
        (fx, fy), _ = axes(which)
        for d in (1, -1):
            recv(f"f{which}{d}", at(which, -d, 0, 0, half))
            src = at(which, -d, 0, part(d), quarter)
            send(f"F{which}{d}", src, at(which, 2, 0, part(d), quarter), dev(fx * d, fy * d))

    def first_last(which):
        for d in (1, -1):
            recv(f"F{which}{d}", at(which, 2, 0, part(d), quarter))

    def second_send(which, a):
        _, (gx, gy) = axes(which)
        for d in (1, -1):
            src, dst = at(which, a, 0, 0, half), at(which, a, -d, 0, half)
            send(f"g{which}{a}{d}", src, dst, dev(gx * d, gy * d))

    def second_forward(which, a):
        _, (gx, gy) = axes(which)
        for d in (1, -1):
            recv(f"g{which}{a}{d}", at(which, a, -d, 0, half))
            src = at(which, a, -d, part(d), quarter)
            send(f"G{which}{a}{d}", src, at(which, a, 2, part(d), quarter), dev(gx * d, gy * d))

    def second_last(which, a):
        for d in (1, -1):
            recv(f"G{which}{a}{d}", at(which, a, 2, part(d), quarter))

    scale = 100.0 * LOG2E

    def tile(t, ic, h=None):
        rows = pl.ds(t * TB if isinstance(t, int) else pl.multiple_of(t * TB, TB), TB)
        width = IB if h is None else IB // 2
        c0 = 0 if h is None else h * width
        cols = slice(c0, c0 + width)
        block = dot_nt(txt[rows, :], img[ic * IB + c0 : ic * IB + c0 + width, :]) * scale
        logit[ic, rows, cols] = block
        deep = block.reshape(TB // 8, 8, width)
        old = imax[ic, :, cols]
        new = jnp.maximum(old, jnp.max(deep, axis=0))
        total = jnp.sum(jnp.exp2(deep - new[None]), axis=0)
        isum[ic, :, cols] = isum[ic, :, cols] * jnp.exp2(old - new) + total
        imax[ic, :, cols] = new
        parts = [block[:, k : k + LANES] for k in range(0, width, LANES)]
        old = tmax[rows, :]
        new = functools.reduce(jnp.maximum, parts, old)
        tsum[rows, :] = functools.reduce(
            lambda a, b: a + b,
            [jnp.exp2(p - new) for p in parts],
            tsum[rows, :] * jnp.exp2(old - new),
        )
        tmax[rows, :] = new

    def tiles(n, at_step):
        def body(i, carry):
            for args in at_step(i):
                tile(*args)
            return carry

        lax.fori_loop(0, n, body, 0)

    n_t = len(order)

    loads[0].wait()
    loads[1].wait()
    own_image, length = project(feats, ihead)
    img[0:pairs, :] = own_image
    pl.semaphore_wait(barrier, len(near))
    for which in (0, 1):
        first_send(which)
    for which in (0, 1):
        second_send(which, 0)
    loads[2].wait()
    loads[3].wait()
    own_text, _ = project(tfeats, thead)
    txt[0:pairs, :] = own_text
    text_send(0, 0)
    text_send(0, 1)
    text_share(0)

    for i in (4, 5, 6, 7):
        loads[i].wait()
    sgne[...] = (2 * signe[...] - 1).astype(jnp.bfloat16)
    norm = jnp.broadcast_to(length, (pairs, LANES)).T[0:1, :]
    izr = dot_nt(sgne[...], own_image)
    own_zr = dot_nt(sgne[...], own_text).astype(jnp.bfloat16).astype(jnp.float32)
    prod = own_image.astype(jnp.float32) * own_text.astype(jnp.float32)
    lanes = functools.reduce(
        lambda a, b: a + b, [prod[:, k : k + LANES] for k in range(0, prod.shape[1], LANES)]
    )
    own_logit = 100.0 * jnp.sum(lanes.T, axis=0, keepdims=True)
    fbuf[...] = dot_nt((2 * signi[...] - 1).astype(jnp.bfloat16), feats[...])
    mine = pl.ds(pl.multiple_of(feat * pairs, pairs), pairs)
    maskall[:, mine] = masks[...].astype(jnp.bfloat16)
    frecv[feat] = fbuf[pl.ds(pl.multiple_of(feat * 8, 8), 8), :]
    tmax[...] = jnp.full(tmax.shape, -1e30, jnp.float32)
    tsum[...] = jnp.zeros(tsum.shape, jnp.float32)
    imax[...] = jnp.full(imax.shape, -1e30, jnp.float32)
    isum[...] = jnp.zeros(isum.shape, jnp.float32)

    for which in (0, 1):
        first_forward(which)
        second_send(which, -1)
        second_send(which, 1)
    for h in (0, 1):
        text_recv(0, h)
        text_send(1, h)
    text_share(1)
    text_share(-1)
    for which in (0, 1):
        second_forward(which, 0)
    for which in (0, 1):
        first_last(which)
        second_send(which, 2)
    for dz in (0, 1, -1):
        text_shared(dz)
    tiles(3, lambda i: [(i, 0)])
    text_recv(1, 0)
    text_send(2, 0)
    text_recv(1, 1)
    text_send(2, 1)
    text_share(2)
    text_share(-2)
    for which in (0, 1):
        for a in (-1, 1):
            second_forward(which, a)
    tiles(3, lambda i: [(i, 1)])
    text_recv(2, 0)
    text_send(3, 0)
    text_shared(2)
    text_shared(-2)
    tiles(2, lambda i: [(i + 3, 0), (i + 3, 1)])
    for which in (0, 1):
        second_last(which, 0)
    tiles(2, lambda i: [(2 * i, 2, 0), (2 * i + 1, 2, 0)])
    text_recv(2, 1)
    text_send(3, 1)
    text_share(3)
    text_share(-3)
    for which in (0, 1):
        second_forward(which, 2)
    text_shared(3)
    text_shared(-3)
    tiles(2, lambda i: [(i + 5, 0), (i + 5, 1)])
    tiles(1, lambda i: [(4, 2, 0), (5, 2, 0), (6, 2, 0)])
    text_recv(3, 0)
    text_recv(3, 1)
    text_share(HZ)
    for which in (0, 1):
        for a in (-1, 1):
            second_last(which, a)
    tiles(n_t - 1, lambda i: [(i, 2, 1), (i, 3, 0)])
    text_shared(HZ)
    tiles(1, lambda i: [(7, 0), (7, 1), (7, 2), (7, 3, 0)])
    for which in (0, 1):
        second_last(which, 2)
    tiles(n_t // 2, lambda i: [(2 * i, 3, 1), (2 * i + 1, 3, 1)])

    for k, (dx, dy) in enumerate(PLANE):
        ic, cols = k // 4, slice(k % 4 * LANES, (k % 4 + 1) * LANES)
        high = imax[ic, :, cols]
        top = jnp.max(high, axis=0, keepdims=True)
        total = jnp.sum(isum[ic, :, cols] * jnp.exp2(high - top), axis=0, keepdims=True)
        rbuf[0, pl.ds(image_slot(dx, dy), 1), :] = top + jnp.log2(total)
    for k, (dx, dy) in enumerate(plane):
        send(f"R{k}", rbuf.at[0], rbuf.at[k + 1], dev(dx, dy))
    texts = [(dz, dc) for dz in order for dc in range(2)]
    for b, (dz, dc) in enumerate(texts):
        rows = slice(b * LANES, (b + 1) * LANES)
        high = tmax[rows, :].T
        top = jnp.max(high, axis=0, keepdims=True)
        total = jnp.sum(tsum[rows, :].T * jnp.exp2(high - top), axis=0, keepdims=True)
        cbuf[0, pl.ds(text_slot(dz, dc), 1), :] = top + jnp.log2(total)
    send("D", cbuf.at[0], cbuf.at[Z], dev(0, 0, 0, 1))
    recv("D", cbuf.at[Z])
    cbuf[Z + 1] = lse2([cbuf[0], cbuf[Z]])
    for k, dz in enumerate(line):
        send(f"C{k}", cbuf.at[Z + 1], cbuf.at[k + 1], dev(0, 0, dz, 0))

    for t in range(n_t // 2):
        rows = slice(t * 2 * TB, (t + 1) * 2 * TB)
        zr[t] = dot_nt(sgne[...], txt[rows, :]).astype(jnp.bfloat16)
    drain()

    for k in range(len(plane)):
        recv(f"R{k}", rbuf.at[k + 1])
    rbuf[0] = lse2([rbuf[k] for k in range(len(plane) + 1)])
    for k, (dx, dy) in enumerate(PLANE):
        cols = slice(k % 4 * LANES, (k % 4 + 1) * LANES)
        rows_lse[k // 4, :, cols] = rbuf[0, pl.ds(image_slot(dx, dy), 1), :]
    for k in range(len(line)):
        recv(f"C{k}", cbuf.at[k + 1])
    cbuf[0] = lse2([cbuf[k] for k in (Z + 1, *range(1, Z))])
    for b, (dz, dc) in enumerate(texts):
        col = cbuf[0, pl.ds(text_slot(dz, dc), 1), :]
        tmax[b * LANES : (b + 1) * LANES, :] = jnp.broadcast_to(col, (LANES, LANES)).T

    for dx, h in mates:
        to = mate(dx, h)
        send(f"m{dx}{h}", maskall.at[:, mine], maskall.at[:, mine], to)
        send(f"r{dx}{h}", fbuf.at[pl.ds(to["feat"] * 8, 8), :], frecv.at[feat], to)

    for ic in (3, 2, 1, 0):
        row = rows_lse[ic]

        def second_pass(t, carry):
            acc, radial = carry
            rows = pl.ds(pl.multiple_of(t * 2 * TB, 2 * TB), 2 * TB)
            block = logit[ic, rows, :]
            col = tmax[rows, :]
            col = jnp.concatenate([col] * (IB // LANES), axis=1)
            weights = (jnp.exp2(block - row) + jnp.exp2(block - col)).astype(jnp.bfloat16)
            acc += jnp.dot(zr[t], weights, preferred_element_type=jnp.float32)
            radial += jnp.sum(
                (weights.astype(jnp.float32) * block).reshape(2 * TB // 8, 8, IB), axis=0
            )
            return acc, radial

        acc, radial = lax.fori_loop(
            0, n_t // 2, second_pass,
            (jnp.zeros((64, IB), jnp.float32), jnp.zeros((8, IB), jnp.float32)),
        )
        for q in range(4):
            k, cols = ic * 4 + q, slice(q * LANES, (q + 1) * LANES)
            msg[k, 0:64, :] = acc[:, cols]
            msg[k, 64:72, :] = radial[:, cols]
            if k > 0:
                send(f"P{k}", msg.at[k], precv.at[k - 1], dev(*PLANE[k]))

    total = msg[0]
    for k in range(len(PLANE) - 1, 0, -1):
        recv(f"P{k}", precv.at[k - 1])
        total += precv[k - 1]
    pulled = 50.0 * total[0:64] - 100.0 * own_zr
    radial = (0.5 / LOG2E) * jnp.sum(total[64:72], axis=0, keepdims=True) - own_logit
    gall[feat] = (pulled - radial * izr) / norm

    for dx, h in mates:
        send(f"g{dx}{h}", gall.at[feat], gall.at[feat], mate(dx, h))
    for dx, h in mates:
        came = mate(-dx, h)["feat"]
        recv(f"m{dx}{h}", maskall.at[:, pl.ds(pl.multiple_of(came * pairs, pairs), pairs)])
        recv(f"r{dx}{h}", frecv.at[came])
    for dx, h in mates:
        recv(f"g{dx}{h}", gall.at[mate(-dx, h)["feat"]])

    shrink = 1.0 / math.sqrt(cfg["vw"])
    for f in range(2 * X):
        g = gall[f]
        for a in range(8):
            phi[a * 64 : (a + 1) * 64, f * pairs : (f + 1) * pairs] = (
                frecv[f, a : a + 1, :] * g * shrink
            ).astype(jnp.bfloat16)
    summed = dot_nt(maskall[...], phi[...])
    high = summed.astype(jnp.bfloat16)
    rest = summed - high.astype(jnp.float32)
    mid = rest.astype(jnp.bfloat16)
    low = (rest - mid.astype(jnp.float32)).astype(jnp.bfloat16)
    tests = tg[...]
    scores = dot_nt(high, tests) + (dot_nt(mid, tests) + dot_nt(low, tests))
    tot[...] = scores.reshape(tot.shape)

    send("core", tot.at[:, :, 1 - c], crecv, dev(0, 0, 0, 1))
    recv("core", crecv)
    both = tot[:, :, c] + crecv[...]
    lane = lax.broadcasted_iota(jnp.int32, (HZ * 8, LANES), 1)
    for ylow in range(2):
        low_z = both[ylow, :HZ].reshape(HZ * 8, -1)
        high_z = both[ylow, HZ:].reshape(HZ * 8, -1)
        for xx in range(X):
            cols = slice(xx * LANES, (xx + 1) * LANES)
            a, b = low_z[:, cols], high_z[:, cols]
            first = jnp.where(lane < 64, a, pltpu.roll(b, 64, 1))
            second = jnp.where(lane < 64, pltpu.roll(a, 64, 1), b)
            pk[xx * Y + ylow] = first.reshape(HZ, 8, LANES)
            pk[xx * Y + 2 + ylow] = second.reshape(HZ, 8, LANES)
    own = image_slot(0, 0)
    for k, (dx, dy) in enumerate(plane):
        send(f"Q{k}", pk.at[image_slot(dx, dy)], prs.at[k], dev(dx, dy))
    total = pk[own]
    for k in range(len(plane)):
        recv(f"Q{k}", prs.at[k])
        total += prs[k]
    acc2[...] = total
    for dz in line:
        dz = dz % Z
        send(f"Z{dz}", acc2.at[zs[dz] & (HZ - 1)], zrs.at[dz - 1], dev(0, 0, dz, 0))
    total = acc2[z & (HZ - 1)]
    for dz in range(1, Z):
        recv(f"Z{dz}", zrs.at[dz - 1])
        total += zrs[dz - 1]
    total = jnp.where(z >= HZ, pltpu.roll(total, 64, 1), total)
    out_ref[...] = total[:, :64] * (1.0 / cfg["divide"])
    drain()


def on_device(*args):
    image_feats, text_feats, image_head, text_head, sign_image, sign_embed, tests, masks = args
    pairs, vw = image_feats.shape
    width = image_head.shape[1]
    Z = lax.axis_size("dp") // 4
    n_devices = lax.axis_size("dp") * lax.axis_size("feat")
    cfg = {"pairs": pairs, "Z": Z, "vw": vw, "divide": math.sqrt(pairs * n_devices * 4096)}
    n_image, n_text = X * Y * pairs, 2 * Z * pairs
    subsets, n_tests = masks.shape[0], tests.shape[0]
    f32, bf16 = jnp.float32, jnp.bfloat16
    vmem = pltpu.VMEM
    operands = (
        image_feats, text_feats, image_head, text_head, sign_image.T, sign_embed.T, masks, tests,
    )
    n_copies = 40 + 4 * Z - 2 + Z + 15 + Z + 15 + 21 + 1 + 15 + Z - 1
    scratch = [vmem(value.shape, value.dtype) for value in operands] + [
        vmem((64, width), bf16),
        vmem((n_image, width), bf16),
        vmem((n_text, width), bf16),
        vmem((X * Y // 4, n_text, 4 * pairs), f32),
        vmem((n_text // (4 * pairs), 64, 4 * pairs), bf16),
        vmem((n_text, LANES), f32),
        vmem((n_text, LANES), f32),
        vmem((X * Y // 4, 8, 4 * pairs), f32),
        vmem((X * Y // 4, 8, 4 * pairs), f32),
        vmem((X * Y, X * Y, pairs), f32),
        vmem((Z + 2, 2 * Z, pairs), f32),
        vmem((X * Y // 4, 1, 4 * pairs), f32),
        vmem((X * Y, 72, pairs), f32),
        vmem((X * Y - 1, 72, pairs), f32),
        vmem((64, pairs), f32),
        vmem((2 * X, 64, pairs), f32),
        vmem((2 * X, 8, pairs), f32),
        vmem((subsets, 2 * X * pairs), bf16),
        vmem((512, 2 * X * pairs), bf16),
        vmem((2, Z, 2, 8, n_tests), f32),
        vmem((2, Z, 8, n_tests), f32),
        vmem((X * Y, Z // 2, 8, LANES), f32),
        vmem((X * Y - 1, Z // 2, 8, LANES), f32),
        vmem((Z // 2, 8, LANES), f32),
        vmem((Z - 1, 8, LANES), f32),
        pltpu.SemaphoreType.DMA((n_copies,)),
        pltpu.SemaphoreType.DMA((n_copies,)),
        pltpu.SemaphoreType.DMA((len(operands),)),
    ]
    return pl.pallas_call(
        functools.partial(kernel, cfg),
        out_shape=jax.ShapeDtypeStruct((8, 64), f32),
        in_specs=[pl.BlockSpec(memory_space=pl.ANY)] * len(operands),
        out_specs=pl.BlockSpec(memory_space=pltpu.VMEM),
        scratch_shapes=scratch,
        compiler_params=pltpu.CompilerParams(
            collective_id=0, has_side_effects=True, vmem_limit_bytes=60 * 1024 * 1024
        ),
    )(*operands)


def solution(mesh):
    placed = (
        P(("dp", "feat"), None),
        P(("dp", "feat"), None),
        P(),
        P(),
        P(),
        P(),
        P(None, "feat"),
        P(None, ("dp", "feat")),
    )
    return jax.shard_map(
        on_device, mesh=mesh, in_specs=placed, out_specs=P("dp", "feat"), check_vma=False
    )
```

```python
import functools
import math

import jax
import jax.numpy as jnp
from jax import lax
from jax.experimental import pallas as pl
from jax.experimental.pallas import tpu as pltpu
from jax.sharding import PartitionSpec as P

X, Y = 4, 4
LANES = 128
LOG2E = math.log2(math.e)
MESH = pl.DeviceIdType.MESH
NT = (((1,), (1,)), ((), ()))


def dot_nt(a, b):
    return lax.dot_general(a, b, NT, preferred_element_type=jnp.float32)


def lse2(parts):
    top = functools.reduce(jnp.maximum, parts)
    total = functools.reduce(lambda a, b: a + b, [jnp.exp2(p - top) for p in parts])
    return top + jnp.log2(total)


class Names:
    def __init__(self):
        self.ids = {}

    def __call__(self, name):
        return self.ids.setdefault(name, len(self.ids))


PLANE = (
    (0, 0), (1, 0), (-1, 0), (0, 1),
    (0, -1), (1, 1), (1, -1), (-1, 1),
    (-1, -1), (2, 0), (0, 2), (2, 1),
    (2, -1), (1, 2), (-1, 2), (2, 2),
)


def kernel(
    cfg,
    feats_hbm, tfeats_hbm, ihead_hbm, thead_hbm, signi_hbm, signe_hbm, mask_hbm, tg_hbm,
    out_ref,
    feats, tfeats, ihead, thead, signi, signe, masks, tg,
    sgne, img, txt, logit, zr, tmax, tsum, imax, isum, rbuf, cbuf, rows_lse, msg, precv,
    fbuf, gmsg, gall, maskall, phi, tot, crecv, pk, prs, acc2, zrs,
    send_sem, recv_sem, load_sem,
):
    pairs, Z, TB = cfg["pairs"], cfg["Z"], 2 * cfg["pairs"]
    IB = 4 * pairs
    half, quarter = pairs // 2, pairs // 4
    HZ = Z // 2
    order = [0] + [d for k in range(1, HZ) for d in (k, -k)] + [HZ]
    dp, feat = lax.axis_index("dp"), lax.axis_index("feat")
    c = dp & 1
    z = (dp >> 1) & (Z - 1)
    yl = dp >> (Z.bit_length())
    x = feat >> 1
    y = ((feat & 1) << 1) + yl

    xs = [(x + d) & (X - 1) for d in range(X)]
    ys = [(y + d) & (Y - 1) for d in range(Y)]
    zs = [(z + d) & (Z - 1) for d in range(Z)]
    cs = [c, 1 - c]
    x_part = [v << 1 for v in xs]
    y_feat = [v >> 1 for v in ys]
    y_dp = [(v & 1) << (Z.bit_length()) for v in ys]
    z_part = [v << 1 for v in zs]

    def dev(dx=0, dy=0, dz=0, dc=0):
        return {
            "dp": y_dp[dy % Y] + z_part[dz % Z] + cs[dc % 2],
            "feat": x_part[dx % X] + y_feat[dy % Y],
        }

    def image_slot(dx, dy):
        return (xs[dx % X] << 2) + ys[dy % Y]

    def text_slot(dz, dc):
        return cs[dc % 2] * Z + zs[dz % Z]

    plane = PLANE[:0:-1]
    line = order[:0:-1]
    mates = [(2, 1), (1, 1), (-1, 1), (2, 0), (0, 1), (1, 0), (-1, 0)]

    def mate(dx, h):
        return {
            "dp": ((yl ^ h) << Z.bit_length()) + z_part[0] + c,
            "feat": x_part[dx % X] + (y_feat[0] ^ h),
        }

    loads = [
        pltpu.make_async_copy(src, dst, load_sem.at[i])
        for i, (src, dst) in enumerate(
            (
                (feats_hbm, feats), (ihead_hbm, ihead), (tfeats_hbm, tfeats),
                (thead_hbm, thead), (signe_hbm, signe), (signi_hbm, signi),
                (mask_hbm, masks), (tg_hbm, tg),
            )
        )
    ]
    for load in loads:
        load.start()

    barrier = pltpu.get_barrier_semaphore()
    near = [(0, 0, 0, 1)]
    for d in (1, -1):
        near += [(d, 0, 0, 0), (0, d, 0, 0), (0, 0, d, 0)]
    for offsets in near:
        pl.semaphore_signal(barrier, inc=1, device_id=dev(*offsets), device_id_type=MESH)

    names = Names()
    started = []

    def send(name, src, dst, to):
        i = names(name)
        copy = pltpu.make_async_remote_copy(
            src_ref=src, dst_ref=dst, send_sem=send_sem.at[i], recv_sem=recv_sem.at[i],
            device_id=to, device_id_type=MESH,
        )
        copy.start()
        started.append(copy)

    def recv(name, dst):
        i = names(name)
        pltpu.make_async_remote_copy(
            src_ref=dst, dst_ref=dst, send_sem=send_sem.at[i], recv_sem=recv_sem.at[i],
            device_id=dev(1), device_id_type=MESH,
        ).wait_recv()

    def drain():
        for copy in started:
            copy.wait_send()
        started.clear()

    def wrap(d, n):
        return (d + n // 2 - 1) % n - (n // 2 - 1)

    def image(dx, dy, r0, n):
        k = PLANE.index((wrap(dx, X), wrap(dy, Y)))
        return img.at[pl.ds(k * pairs + r0, n), :]

    def text(dz, dc, r0, n):
        k = order.index(wrap(dz, Z)) * 2 + dc % 2
        return txt.at[pl.ds(k * pairs + r0, n), :]

    def project(feats_ref, head_ref):
        proj = jnp.dot(feats_ref[...], head_ref[...], preferred_element_type=jnp.float32)
        length = jnp.sqrt(jnp.sum(proj * proj, axis=1, keepdims=True) + 1e-06)
        return (proj / length).astype(jnp.bfloat16), length

    def text_pieces(s, up):
        if s < HZ - 1:
            return (0, 1, 2, 3)
        return (0, 1) if up else (2, 3)

    def text_send(s, q):
        for up, step in ((True, 1), (False, -1)):
            if q in text_pieces(s, up):
                src = text(-s * step, 0, q * quarter, quarter)
                dst = text(-(s + 1) * step, 0, q * quarter, quarter)
                send(f"z{step}{s}{q}", src, dst, dev(0, 0, step, 0))

    def text_recv(s, q):
        for up, step in ((True, 1), (False, -1)):
            if q in text_pieces(s, up):
                recv(f"z{step}{s}{q}", text(-(s + 1) * step, 0, q * quarter, quarter))

    def text_next(s, *qs):
        for q in qs:
            text_recv(s, q)
            text_send(s + 1, q)

    def text_share(dz):
        send(f"s{dz}", text(dz, 0, 0, pairs), text(dz, 1, 0, pairs), dev(0, 0, 0, 1))

    def text_shared(dz):
        recv(f"s{dz}", text(dz, 1, 0, pairs))

    def axes(which):
        return ((1, 0), (0, 1)) if which == 0 else ((0, 1), (1, 0))

    def at(which, a, b, r0, n):
        (fx, fy), (gx, gy) = axes(which)
        return image(fx * a + gx * b, fy * a + gy * b, which * half + r0, n)

    def part(d):
        return 0 if d == 1 else quarter

    def first_send(which):
        (fx, fy), _ = axes(which)
        for d in (1, -1):
            src, dst = at(which, 0, 0, 0, half), at(which, -d, 0, 0, half)
            send(f"f{which}{d}", src, dst, dev(fx * d, fy * d))

    def first_forward(which):
        (fx, fy), _ = axes(which)
        for d in (1, -1):
            recv(f"f{which}{d}", at(which, -d, 0, 0, half))
            src = at(which, -d, 0, part(d), quarter)
            send(f"F{which}{d}", src, at(which, 2, 0, part(d), quarter), dev(fx * d, fy * d))

    def first_last(which):
        for d in (1, -1):
            recv(f"F{which}{d}", at(which, 2, 0, part(d), quarter))

    def second_send(which, a):
        _, (gx, gy) = axes(which)
        for d in (1, -1):
            src, dst = at(which, a, 0, 0, half), at(which, a, -d, 0, half)
            send(f"g{which}{a}{d}", src, dst, dev(gx * d, gy * d))

    def second_forward(which, a):
        _, (gx, gy) = axes(which)
        for d in (1, -1):
            recv(f"g{which}{a}{d}", at(which, a, -d, 0, half))
            src = at(which, a, -d, part(d), quarter)
            send(f"G{which}{a}{d}", src, at(which, a, 2, part(d), quarter), dev(gx * d, gy * d))

    def second_last(which, a):
        for d in (1, -1):
            recv(f"G{which}{a}{d}", at(which, a, 2, part(d), quarter))

    scale = 100.0 * LOG2E

    def tile(t, ic, h=None):
        rows = pl.ds(t * TB if isinstance(t, int) else pl.multiple_of(t * TB, TB), TB)
        width = IB if h is None else IB // 2
        c0 = 0 if h is None else h * width
        cols = slice(c0, c0 + width)
        block = dot_nt(txt[rows, :], img[ic * IB + c0 : ic * IB + c0 + width, :]) * scale
        logit[ic, rows, cols] = block
        deep = block.reshape(TB // 8, 8, width)
        old = imax[ic, :, cols]
        new = jnp.maximum(old, jnp.max(deep, axis=0))
        total = jnp.sum(jnp.exp2(deep - new[None]), axis=0)
        isum[ic, :, cols] = isum[ic, :, cols] * jnp.exp2(old - new) + total
        imax[ic, :, cols] = new
        parts = [block[:, k : k + LANES] for k in range(0, width, LANES)]
        old = tmax[rows, :]
        new = functools.reduce(jnp.maximum, parts, old)
        tsum[rows, :] = functools.reduce(
            lambda a, b: a + b,
            [jnp.exp2(p - new) for p in parts],
            tsum[rows, :] * jnp.exp2(old - new),
        )
        tmax[rows, :] = new

    def tiles(n, at_step):
        def body(i, carry):
            for args in at_step(i):
                tile(*args)
            return carry

        lax.fori_loop(0, n, body, 0)

    n_t = len(order)

    loads[0].wait()
    loads[1].wait()
    own_image, length = project(feats, ihead)
    img[0:pairs, :] = own_image
    pl.semaphore_wait(barrier, len(near))
    for which in (0, 1):
        first_send(which)
    for which in (0, 1):
        second_send(which, 0)
    loads[2].wait()
    loads[3].wait()
    own_text, _ = project(tfeats, thead)
    txt[0:pairs, :] = own_text
    for q in range(4):
        text_send(0, q)
    text_share(0)

    for i in (4, 5, 6, 7):
        loads[i].wait()
    sgne[...] = (2 * signe[...] - 1).astype(jnp.bfloat16)
    norm = jnp.broadcast_to(length, (pairs, LANES)).T[0:1, :]
    izr = dot_nt(sgne[...], own_image)
    own_zr = dot_nt(sgne[...], own_text).astype(jnp.bfloat16).astype(jnp.float32)
    prod = own_image.astype(jnp.float32) * own_text.astype(jnp.float32)
    lanes = functools.reduce(
        lambda a, b: a + b, [prod[:, k : k + LANES] for k in range(0, prod.shape[1], LANES)]
    )
    own_logit = 100.0 * jnp.sum(lanes.T, axis=0, keepdims=True)
    fbuf[...] = dot_nt((2 * signi[...] - 1).astype(jnp.bfloat16), feats[...])
    mine = pl.ds(pl.multiple_of(feat * pairs, pairs), pairs)
    maskall[:, mine] = masks[...].astype(jnp.bfloat16)
    tmax[...] = jnp.full(tmax.shape, -1e30, jnp.float32)
    tsum[...] = jnp.zeros(tsum.shape, jnp.float32)
    imax[...] = jnp.full(imax.shape, -1e30, jnp.float32)
    isum[...] = jnp.zeros(isum.shape, jnp.float32)

    for which in (0, 1):
        first_forward(which)
        second_send(which, -1)
        second_send(which, 1)
    text_next(0, 0, 1)
    for which in (0, 1):
        second_forward(which, 0)
    text_next(0, 2)
    for which in (0, 1):
        first_last(which)
        second_send(which, 2)
    text_next(0, 3)
    text_share(1)
    text_share(-1)
    text_next(1, 0)
    for dz in (0, 1, -1):
        text_shared(dz)
    tiles(1, lambda i: [(0, 0), (1, 0), (2, 0)])
    text_next(1, 1)
    for which in (0, 1):
        second_forward(which, -1)
    text_next(1, 2)
    for which in (0, 1):
        second_forward(which, 1)
    text_next(1, 3)
    text_share(2)
    text_share(-2)
    tiles(1, lambda i: [(0, 1), (1, 1), (2, 1)])
    text_next(2, 0)
    text_shared(2)
    text_shared(-2)
    tiles(1, lambda i: [(3, 0), (3, 1), (4, 0), (4, 1)])
    text_next(2, 1)
    for which in (0, 1):
        second_forward(which, 2)
    for which in (0, 1):
        second_last(which, 0)
    text_next(2, 2)
    tiles(1, lambda i: [(t, 2, 0) for t in range(5)])
    text_next(2, 3)
    text_share(3)
    text_share(-3)
    for dx, h in mates:
        send(f"m{dx}{h}", maskall.at[:, mine], maskall.at[:, mine], mate(dx, h))
    for which in (0, 1):
        for a in (-1, 1):
            second_last(which, a)
    tiles(5, lambda i: [(i, 2, 1), (i, 3, 0)])
    for q in range(4):
        text_recv(HZ - 1, q)
    text_share(HZ)
    text_shared(3)
    text_shared(-3)
    tiles(2, lambda i: [(i + 5, 0), (i + 5, 1), (i + 5, 2), (i + 5, 3, 0)])
    for which in (0, 1):
        second_last(which, 2)
    tiles(1, lambda i: [(t, 3, 1) for t in range(7)])
    text_shared(HZ)
    tiles(1, lambda i: [(7, 0), (7, 1), (7, 2), (7, 3)])

    for k, (dx, dy) in enumerate(PLANE):
        ic, cols = k // 4, slice(k % 4 * LANES, (k % 4 + 1) * LANES)
        high = imax[ic, :, cols]
        top = jnp.max(high, axis=0, keepdims=True)
        total = jnp.sum(isum[ic, :, cols] * jnp.exp2(high - top), axis=0, keepdims=True)
        rbuf[0, pl.ds(image_slot(dx, dy), 1), :] = top + jnp.log2(total)
    for k, (dx, dy) in enumerate(plane):
        send(f"R{k}", rbuf.at[0], rbuf.at[k + 1], dev(dx, dy))
    texts = [(dz, dc) for dz in order for dc in range(2)]
    for b, (dz, dc) in enumerate(texts):
        rows = slice(b * LANES, (b + 1) * LANES)
        high = tmax[rows, :].T
        top = jnp.max(high, axis=0, keepdims=True)
        total = jnp.sum(tsum[rows, :].T * jnp.exp2(high - top), axis=0, keepdims=True)
        cbuf[0, pl.ds(text_slot(dz, dc), 1), :] = top + jnp.log2(total)
    send("D", cbuf.at[0], cbuf.at[Z], dev(0, 0, 0, 1))
    recv("D", cbuf.at[Z])
    cbuf[Z + 1] = lse2([cbuf[0], cbuf[Z]])
    for k, dz in enumerate(line):
        send(f"C{k}", cbuf.at[Z + 1], cbuf.at[k + 1], dev(0, 0, dz, 0))

    for t in range(n_t // 2):
        rows = slice(t * 2 * TB, (t + 1) * 2 * TB)
        zr[t] = dot_nt(sgne[...], txt[rows, :]).astype(jnp.bfloat16)
    drain()

    for k in range(len(plane)):
        recv(f"R{k}", rbuf.at[k + 1])
    rbuf[0] = lse2([rbuf[k] for k in range(len(plane) + 1)])
    for k, (dx, dy) in enumerate(PLANE):
        cols = slice(k % 4 * LANES, (k % 4 + 1) * LANES)
        rows_lse[k // 4, :, cols] = rbuf[0, pl.ds(image_slot(dx, dy), 1), :]
    for k in range(len(line)):
        recv(f"C{k}", cbuf.at[k + 1])
    cbuf[0] = lse2([cbuf[k] for k in (Z + 1, *range(1, Z))])
    for b, (dz, dc) in enumerate(texts):
        col = cbuf[0, pl.ds(text_slot(dz, dc), 1), :]
        tmax[b * LANES : (b + 1) * LANES, :] = jnp.broadcast_to(col, (LANES, LANES)).T

    for ic in (3, 2, 1, 0):
        row = rows_lse[ic]

        def second_pass(t, carry):
            acc, radial = carry
            rows = pl.ds(pl.multiple_of(t * 2 * TB, 2 * TB), 2 * TB)
            block = logit[ic, rows, :]
            col = tmax[rows, :]
            col = jnp.concatenate([col] * (IB // LANES), axis=1)
            weights = (jnp.exp2(block - row) + jnp.exp2(block - col)).astype(jnp.bfloat16)
            acc += jnp.dot(zr[t], weights, preferred_element_type=jnp.float32)
            radial += jnp.sum(
                (weights.astype(jnp.float32) * block).reshape(2 * TB // 8, 8, IB), axis=0
            )
            return acc, radial

        acc, radial = lax.fori_loop(
            0, n_t // 2, second_pass,
            (jnp.zeros((64, IB), jnp.float32), jnp.zeros((8, IB), jnp.float32)),
        )
        for q in range(4):
            k, cols = ic * 4 + q, slice(q * LANES, (q + 1) * LANES)
            msg[k, 0:64, :] = acc[:, cols]
            msg[k, 64:72, :] = radial[:, cols]
            if k > 0:
                send(f"P{k}", msg.at[k], precv.at[k - 1], dev(*PLANE[k]))

    total = msg[0]
    for k in range(len(PLANE) - 1, 0, -1):
        recv(f"P{k}", precv.at[k - 1])
        total += precv[k - 1]
    pulled = 50.0 * total[0:64] - 100.0 * own_zr
    radial = (0.5 / LOG2E) * jnp.sum(total[64:72], axis=0, keepdims=True) - own_logit
    grad = (pulled - radial * izr) / norm

    def with_features(to):
        return jnp.concatenate([grad, fbuf[pl.ds(pl.multiple_of(to * 8, 8), 8), :]], axis=0)

    for k, (dx, h) in enumerate(mates):
        to = mate(dx, h)
        gmsg[k] = with_features(to["feat"])
        send(f"g{dx}{h}", gmsg.at[k], gall.at[feat], to)
    gall[feat] = with_features(feat)
    for dx, h in mates:
        came = mate(-dx, h)["feat"]
        recv(f"m{dx}{h}", maskall.at[:, pl.ds(pl.multiple_of(came * pairs, pairs), pairs)])
    for dx, h in mates:
        recv(f"g{dx}{h}", gall.at[mate(-dx, h)["feat"]])

    shrink = 1.0 / math.sqrt(cfg["vw"])
    for f in range(2 * X):
        g = gall[f, 0:64]
        for a in range(8):
            phi[a * 64 : (a + 1) * 64, f * pairs : (f + 1) * pairs] = (
                gall[f, 64 + a : 65 + a, :] * g * shrink
            ).astype(jnp.bfloat16)
    summed = dot_nt(maskall[...], phi[...])
    high = summed.astype(jnp.bfloat16)
    rest = summed - high.astype(jnp.float32)
    mid = rest.astype(jnp.bfloat16)
    low = (rest - mid.astype(jnp.float32)).astype(jnp.bfloat16)
    tests = tg[...]
    scores = dot_nt(high, tests) + (dot_nt(mid, tests) + dot_nt(low, tests))
    tot[...] = scores.reshape(tot.shape)

    send("core", tot.at[:, :, 1 - c], crecv, dev(0, 0, 0, 1))
    recv("core", crecv)
    both = tot[:, :, c] + crecv[...]
    lane = lax.broadcasted_iota(jnp.int32, (HZ * 8, LANES), 1)
    for ylow in range(2):
        low_z = both[ylow, :HZ].reshape(HZ * 8, -1)
        high_z = both[ylow, HZ:].reshape(HZ * 8, -1)
        for xx in range(X):
            cols = slice(xx * LANES, (xx + 1) * LANES)
            a, b = low_z[:, cols], high_z[:, cols]
            first = jnp.where(lane < 64, a, pltpu.roll(b, 64, 1))
            second = jnp.where(lane < 64, pltpu.roll(a, 64, 1), b)
            pk[xx * Y + ylow] = first.reshape(HZ, 8, LANES)
            pk[xx * Y + 2 + ylow] = second.reshape(HZ, 8, LANES)
    own = image_slot(0, 0)
    for k, (dx, dy) in enumerate(plane):
        send(f"Q{k}", pk.at[image_slot(dx, dy)], prs.at[k], dev(dx, dy))
    total = pk[own]
    for k in range(len(plane)):
        recv(f"Q{k}", prs.at[k])
        total += prs[k]
    acc2[...] = total
    for dz in line:
        dz = dz % Z
        send(f"Z{dz}", acc2.at[zs[dz] & (HZ - 1)], zrs.at[dz - 1], dev(0, 0, dz, 0))
    total = acc2[z & (HZ - 1)]
    for dz in range(1, Z):
        recv(f"Z{dz}", zrs.at[dz - 1])
        total += zrs[dz - 1]
    total = jnp.where(z >= HZ, pltpu.roll(total, 64, 1), total)
    out_ref[...] = total[:, :64] * (1.0 / cfg["divide"])
    drain()


def on_device(*args):
    image_feats, text_feats, image_head, text_head, sign_image, sign_embed, tests, masks = args
    pairs, vw = image_feats.shape
    width = image_head.shape[1]
    Z = lax.axis_size("dp") // 4
    n_devices = lax.axis_size("dp") * lax.axis_size("feat")
    cfg = {"pairs": pairs, "Z": Z, "vw": vw, "divide": math.sqrt(pairs * n_devices * 4096)}
    n_image, n_text = X * Y * pairs, 2 * Z * pairs
    subsets, n_tests = masks.shape[0], tests.shape[0]
    f32, bf16 = jnp.float32, jnp.bfloat16
    vmem = pltpu.VMEM
    operands = (
        image_feats, text_feats, image_head, text_head, sign_image.T, sign_embed.T, masks, tests,
    )
    n_copies = 40 + 4 * Z - 4 + Z + 15 + Z + 15 + 14 + 1 + 15 + Z - 1
    scratch = [vmem(value.shape, value.dtype) for value in operands] + [
        vmem((64, width), bf16),
        vmem((n_image, width), bf16),
        vmem((n_text, width), bf16),
        vmem((X * Y // 4, n_text, 4 * pairs), f32),
        vmem((n_text // (4 * pairs), 64, 4 * pairs), bf16),
        vmem((n_text, LANES), f32),
        vmem((n_text, LANES), f32),
        vmem((X * Y // 4, 8, 4 * pairs), f32),
        vmem((X * Y // 4, 8, 4 * pairs), f32),
        vmem((X * Y, X * Y, pairs), f32),
        vmem((Z + 2, 2 * Z, pairs), f32),
        vmem((X * Y // 4, 1, 4 * pairs), f32),
        vmem((X * Y, 72, pairs), f32),
        vmem((X * Y - 1, 72, pairs), f32),
        vmem((64, pairs), f32),
        vmem((2 * X - 1, 72, pairs), f32),
        vmem((2 * X, 72, pairs), f32),
        vmem((subsets, 2 * X * pairs), bf16),
        vmem((512, 2 * X * pairs), bf16),
        vmem((2, Z, 2, 8, n_tests), f32),
        vmem((2, Z, 8, n_tests), f32),
        vmem((X * Y, Z // 2, 8, LANES), f32),
        vmem((X * Y - 1, Z // 2, 8, LANES), f32),
        vmem((Z // 2, 8, LANES), f32),
        vmem((Z - 1, 8, LANES), f32),
        pltpu.SemaphoreType.DMA((n_copies,)),
        pltpu.SemaphoreType.DMA((n_copies,)),
        pltpu.SemaphoreType.DMA((len(operands),)),
    ]
    return pl.pallas_call(
        functools.partial(kernel, cfg),
        out_shape=jax.ShapeDtypeStruct((8, 64), f32),
        in_specs=[pl.BlockSpec(memory_space=pl.ANY)] * len(operands),
        out_specs=pl.BlockSpec(memory_space=pltpu.VMEM),
        scratch_shapes=scratch,
        compiler_params=pltpu.CompilerParams(
            collective_id=0, has_side_effects=True, vmem_limit_bytes=60 * 1024 * 1024
        ),
    )(*operands)


def solution(mesh):
    placed = (
        P(("dp", "feat"), None),
        P(("dp", "feat"), None),
        P(),
        P(),
        P(),
        P(),
        P(None, "feat"),
        P(None, ("dp", "feat")),
    )
    return jax.shard_map(
        on_device, mesh=mesh, in_specs=placed, out_specs=P("dp", "feat"), check_vma=False
    )
```

```python
import functools
import math

import jax
import jax.numpy as jnp
from jax import lax
from jax.experimental import pallas as pl
from jax.experimental.pallas import tpu as pltpu
from jax.sharding import PartitionSpec as P

X, Y = 4, 4
LANES = 128
LOG2E = math.log2(math.e)
MESH = pl.DeviceIdType.MESH
NT = (((1,), (1,)), ((), ()))


def dot_nt(a, b):
    return lax.dot_general(a, b, NT, preferred_element_type=jnp.float32)


def lse2(parts):
    top = functools.reduce(jnp.maximum, parts)
    total = functools.reduce(lambda a, b: a + b, [jnp.exp2(p - top) for p in parts])
    return top + jnp.log2(total)


class Names:
    def __init__(self):
        self.ids = {}

    def __call__(self, name):
        return self.ids.setdefault(name, len(self.ids))


PLANE = (
    (0, 0), (1, 0), (-1, 0), (0, 1),
    (0, -1), (1, 1), (1, -1), (-1, 1),
    (-1, -1), (2, 0), (0, 2), (2, 1),
    (2, -1), (1, 2), (-1, 2), (2, 2),
)


def kernel(
    cfg,
    feats_hbm, tfeats_hbm, ihead_hbm, thead_hbm, signi_hbm, signe_hbm, mask_hbm, tg_hbm,
    out_ref,
    feats, tfeats, ihead, thead, signi, signe, masks, tg,
    sgne, img, txt, logit, zr, tmax, tsum, imax, isum, rbuf, cbuf, rows_lse, msg, precv,
    fbuf, gmsg, gall, maskall, phi, tot, crecv, pk, prs, acc2, zrs,
    send_sem, recv_sem, load_sem,
):
    pairs, Z, TB = cfg["pairs"], cfg["Z"], 2 * cfg["pairs"]
    IB = 4 * pairs
    half, quarter = pairs // 2, pairs // 4
    HZ = Z // 2
    order = [0] + [d for k in range(1, HZ) for d in (k, -k)] + [HZ]
    dp, feat = lax.axis_index("dp"), lax.axis_index("feat")
    c = dp & 1
    z = (dp >> 1) & (Z - 1)
    yl = dp >> (Z.bit_length())
    x = feat >> 1
    y = ((feat & 1) << 1) + yl

    xs = [(x + d) & (X - 1) for d in range(X)]
    ys = [(y + d) & (Y - 1) for d in range(Y)]
    zs = [(z + d) & (Z - 1) for d in range(Z)]
    cs = [c, 1 - c]
    x_part = [v << 1 for v in xs]
    y_feat = [v >> 1 for v in ys]
    y_dp = [(v & 1) << (Z.bit_length()) for v in ys]
    z_part = [v << 1 for v in zs]

    def dev(dx=0, dy=0, dz=0, dc=0):
        return {
            "dp": y_dp[dy % Y] + z_part[dz % Z] + cs[dc % 2],
            "feat": x_part[dx % X] + y_feat[dy % Y],
        }

    def image_slot(dx, dy):
        return (xs[dx % X] << 2) + ys[dy % Y]

    def text_slot(dz, dc):
        return cs[dc % 2] * Z + zs[dz % Z]

    plane = PLANE[:0:-1]
    line = order[:0:-1]
    mates = [(2, 1), (1, 1), (-1, 1), (2, 0), (0, 1), (1, 0), (-1, 0)]

    def mate(dx, h):
        return {
            "dp": ((yl ^ h) << Z.bit_length()) + z_part[0] + c,
            "feat": x_part[dx % X] + (y_feat[0] ^ h),
        }

    loads = []

    def load(src, dst):
        copy = pltpu.make_async_copy(src, dst, load_sem.at[len(loads)])
        copy.start()
        loads.append(copy)
        return copy

    def load_head(src, dst):
        depth = src.shape[0]
        cuts = [0, 3 * LANES, 6 * LANES, 9 * LANES, depth]
        return [
            (load(src.at[a:b, :], dst.at[a:b, :]), a, b)
            for a, b in zip(cuts, cuts[1:])
            if a < b
        ]

    feats_load = load(feats_hbm, feats)
    ihead_loads = load_head(ihead_hbm, ihead)

    barrier = pltpu.get_barrier_semaphore()
    near = [(0, 0, 0, 1)]
    for d in (1, -1):
        near += [(d, 0, 0, 0), (0, d, 0, 0), (0, 0, d, 0)]
    for offsets in near:
        pl.semaphore_signal(barrier, inc=1, device_id=dev(*offsets), device_id_type=MESH)

    tfeats_load = load(tfeats_hbm, tfeats)
    thead_loads = load_head(thead_hbm, thead)
    other_loads = [
        load(signe_hbm, signe), load(signi_hbm, signi), load(mask_hbm, masks), load(tg_hbm, tg)
    ]

    names = Names()
    started = []

    def send(name, src, dst, to):
        i = names(name)
        copy = pltpu.make_async_remote_copy(
            src_ref=src, dst_ref=dst, send_sem=send_sem.at[i], recv_sem=recv_sem.at[i],
            device_id=to, device_id_type=MESH,
        )
        copy.start()
        started.append(copy)

    def recv(name, dst):
        i = names(name)
        pltpu.make_async_remote_copy(
            src_ref=dst, dst_ref=dst, send_sem=send_sem.at[i], recv_sem=recv_sem.at[i],
            device_id=dev(1), device_id_type=MESH,
        ).wait_recv()

    def drain():
        for copy in started:
            copy.wait_send()
        started.clear()

    def wrap(d, n):
        return (d + n // 2 - 1) % n - (n // 2 - 1)

    def image(dx, dy, r0, n):
        k = PLANE.index((wrap(dx, X), wrap(dy, Y)))
        return img.at[pl.ds(k * pairs + r0, n), :]

    def text(dz, dc, r0, n):
        k = order.index(wrap(dz, Z)) * 2 + dc % 2
        return txt.at[pl.ds(k * pairs + r0, n), :]

    def project(feats_load, feats_ref, head_loads, head_ref):
        feats_load.wait()
        proj = None
        for copy, a, b in head_loads:
            copy.wait()
            term = jnp.dot(
                feats_ref[:, a:b], head_ref[a:b, :], preferred_element_type=jnp.float32
            )
            proj = term if proj is None else proj + term
        length = jnp.sqrt(jnp.sum(proj * proj, axis=1, keepdims=True) + 1e-06)
        return (proj / length).astype(jnp.bfloat16), length

    def text_pieces(s, up):
        if s < HZ - 1:
            return (0, 1, 2, 3)
        return (0, 1) if up else (2, 3)

    def text_send(s, q):
        for up, step in ((True, 1), (False, -1)):
            if q in text_pieces(s, up):
                src = text(-s * step, 0, q * quarter, quarter)
                dst = text(-(s + 1) * step, 0, q * quarter, quarter)
                send(f"z{step}{s}{q}", src, dst, dev(0, 0, step, 0))

    def text_recv(s, q):
        for up, step in ((True, 1), (False, -1)):
            if q in text_pieces(s, up):
                recv(f"z{step}{s}{q}", text(-(s + 1) * step, 0, q * quarter, quarter))

    def text_next(s, *qs):
        for q in qs:
            text_recv(s, q)
            text_send(s + 1, q)

    def text_share(dz):
        send(f"s{dz}", text(dz, 0, 0, pairs), text(dz, 1, 0, pairs), dev(0, 0, 0, 1))

    def text_shared(dz):
        recv(f"s{dz}", text(dz, 1, 0, pairs))

    def axes(which):
        return ((1, 0), (0, 1)) if which == 0 else ((0, 1), (1, 0))

    def at(which, a, b, r0, n):
        (fx, fy), (gx, gy) = axes(which)
        return image(fx * a + gx * b, fy * a + gy * b, which * half + r0, n)

    def part(d):
        return 0 if d == 1 else quarter

    def first_send(which):
        (fx, fy), _ = axes(which)
        for d in (1, -1):
            src, dst = at(which, 0, 0, 0, half), at(which, -d, 0, 0, half)
            send(f"f{which}{d}", src, dst, dev(fx * d, fy * d))

    def first_forward(which):
        (fx, fy), _ = axes(which)
        for d in (1, -1):
            recv(f"f{which}{d}", at(which, -d, 0, 0, half))
            src = at(which, -d, 0, part(d), quarter)
            send(f"F{which}{d}", src, at(which, 2, 0, part(d), quarter), dev(fx * d, fy * d))

    def first_last(which):
        for d in (1, -1):
            recv(f"F{which}{d}", at(which, 2, 0, part(d), quarter))

    def second_send(which, a):
        _, (gx, gy) = axes(which)
        for d in (1, -1):
            src, dst = at(which, a, 0, 0, half), at(which, a, -d, 0, half)
            send(f"g{which}{a}{d}", src, dst, dev(gx * d, gy * d))

    def second_forward(which, a):
        _, (gx, gy) = axes(which)
        for d in (1, -1):
            recv(f"g{which}{a}{d}", at(which, a, -d, 0, half))
            src = at(which, a, -d, part(d), quarter)
            send(f"G{which}{a}{d}", src, at(which, a, 2, part(d), quarter), dev(gx * d, gy * d))

    def second_last(which, a):
        for d in (1, -1):
            recv(f"G{which}{a}{d}", at(which, a, 2, part(d), quarter))

    scale = 100.0 * LOG2E

    def tile(t, n, ic, h=None):
        rows = slice(t * TB, (t + n) * TB)
        width = IB if h is None else IB // 2
        c0 = 0 if h is None else h * width
        cols = slice(c0, c0 + width)
        block = dot_nt(txt[rows, :], img[ic * IB + c0 : ic * IB + c0 + width, :]) * scale
        logit[ic, rows, cols] = block
        deep = block.reshape(n * TB // 8, 8, width)
        old = imax[ic, :, cols]
        new = jnp.maximum(old, jnp.max(deep, axis=0))
        total = jnp.sum(jnp.exp2(deep - new[None]), axis=0)
        isum[ic, :, cols] = isum[ic, :, cols] * jnp.exp2(old - new) + total
        imax[ic, :, cols] = new
        parts = [block[:, k : k + LANES] for k in range(0, width, LANES)]
        old = tmax[rows, :]
        new = functools.reduce(jnp.maximum, parts, old)
        tsum[rows, :] = functools.reduce(
            lambda a, b: a + b,
            [jnp.exp2(p - new) for p in parts],
            tsum[rows, :] * jnp.exp2(old - new),
        )
        tmax[rows, :] = new

    def tiles(*steps):
        for step in steps:
            tile(*step)

    n_t = len(order)

    own_image, length = project(feats_load, feats, ihead_loads, ihead)
    img[0:pairs, :] = own_image
    pl.semaphore_wait(barrier, len(near))
    for which in (0, 1):
        first_send(which)
    for which in (0, 1):
        second_send(which, 0)
    own_text, _ = project(tfeats_load, tfeats, thead_loads, thead)
    txt[0:pairs, :] = own_text
    for q in range(4):
        text_send(0, q)
    text_share(0)

    for copy in other_loads:
        copy.wait()
    sgne[...] = (2 * signe[...] - 1).astype(jnp.bfloat16)
    norm = jnp.broadcast_to(length, (pairs, LANES)).T[0:1, :]
    izr = dot_nt(sgne[...], own_image)
    own_zr = dot_nt(sgne[...], own_text).astype(jnp.bfloat16).astype(jnp.float32)
    prod = own_image.astype(jnp.float32) * own_text.astype(jnp.float32)
    lanes = functools.reduce(
        lambda a, b: a + b, [prod[:, k : k + LANES] for k in range(0, prod.shape[1], LANES)]
    )
    own_logit = 100.0 * jnp.sum(lanes.T, axis=0, keepdims=True)
    fbuf[...] = dot_nt((2 * signi[...] - 1).astype(jnp.bfloat16), feats[...])
    mine = pl.ds(pl.multiple_of(feat * pairs, pairs), pairs)
    maskall[:, mine] = masks[...].astype(jnp.bfloat16)
    tmax[...] = jnp.full(tmax.shape, -1e30, jnp.float32)
    tsum[...] = jnp.zeros(tsum.shape, jnp.float32)
    imax[...] = jnp.full(imax.shape, -1e30, jnp.float32)
    isum[...] = jnp.zeros(isum.shape, jnp.float32)

    for which in (0, 1):
        first_forward(which)
        second_send(which, -1)
        second_send(which, 1)
    text_next(0, 0, 1)
    for which in (0, 1):
        second_forward(which, 0)
    text_next(0, 2)
    for which in (0, 1):
        first_last(which)
        second_send(which, 2)
    text_next(0, 3)
    text_share(1)
    text_share(-1)
    text_next(1, 0)
    for dz in (0, 1, -1):
        text_shared(dz)
    tiles((0, 1, 0), (1, 1, 0), (2, 1, 0))
    text_next(1, 1)
    for which in (0, 1):
        second_forward(which, -1)
    text_next(1, 2)
    for which in (0, 1):
        second_forward(which, 1)
    text_next(1, 3)
    text_share(2)
    text_share(-2)
    tiles((0, 1, 1), (1, 1, 1), (2, 1, 1))
    text_next(2, 0)
    text_shared(2)
    text_shared(-2)
    tiles((3, 1, 0), (3, 1, 1), (4, 1, 0), (4, 1, 1))
    text_next(2, 1)
    for which in (0, 1):
        second_forward(which, 2)
    for which in (0, 1):
        second_last(which, 0)
    text_next(2, 2)
    tiles((0, 2, 2, 0), (2, 3, 2, 0))
    text_next(2, 3)
    text_share(3)
    text_share(-3)
    for dx, h in mates:
        send(f"m{dx}{h}", maskall.at[:, mine], maskall.at[:, mine], mate(dx, h))
    for which in (0, 1):
        for a in (-1, 1):
            second_last(which, a)
    tiles((0, 2, 2, 1), (2, 3, 2, 1), (0, 2, 3, 0), (2, 3, 3, 0))
    for q in range(4):
        text_recv(HZ - 1, q)
    text_share(HZ)
    text_shared(3)
    text_shared(-3)
    tiles(*[(t, 1, ic) for t in (5, 6) for ic in range(3)], (5, 2, 3, 0))
    for which in (0, 1):
        second_last(which, 2)
    text_shared(HZ)
    tiles((7, 1, 0), (7, 1, 1), (7, 1, 2), (7, 1, 3))
    tiles((0, 2, 3, 1), (2, 2, 3, 1), (4, 3, 3, 1))

    for k, (dx, dy) in enumerate(PLANE):
        ic, cols = k // 4, slice(k % 4 * LANES, (k % 4 + 1) * LANES)
        high = imax[ic, :, cols]
        top = jnp.max(high, axis=0, keepdims=True)
        total = jnp.sum(isum[ic, :, cols] * jnp.exp2(high - top), axis=0, keepdims=True)
        rbuf[0, pl.ds(image_slot(dx, dy), 1), :] = top + jnp.log2(total)
    for k, (dx, dy) in enumerate(plane):
        send(f"R{k}", rbuf.at[0], rbuf.at[k + 1], dev(dx, dy))
    texts = [(dz, dc) for dz in order for dc in range(2)]
    for b, (dz, dc) in enumerate(texts):
        rows = slice(b * LANES, (b + 1) * LANES)
        high = tmax[rows, :].T
        top = jnp.max(high, axis=0, keepdims=True)
        total = jnp.sum(tsum[rows, :].T * jnp.exp2(high - top), axis=0, keepdims=True)
        cbuf[0, pl.ds(text_slot(dz, dc), 1), :] = top + jnp.log2(total)
    send("D", cbuf.at[0], cbuf.at[Z], dev(0, 0, 0, 1))
    recv("D", cbuf.at[Z])
    cbuf[Z + 1] = lse2([cbuf[0], cbuf[Z]])
    for k, dz in enumerate(line):
        send(f"C{k}", cbuf.at[Z + 1], cbuf.at[k + 1], dev(0, 0, dz, 0))

    for t in range(n_t // 2):
        rows = slice(t * 2 * TB, (t + 1) * 2 * TB)
        zr[t] = dot_nt(sgne[...], txt[rows, :]).astype(jnp.bfloat16)
    drain()

    for k in range(len(plane)):
        recv(f"R{k}", rbuf.at[k + 1])
    rbuf[0] = lse2([rbuf[k] for k in range(len(plane) + 1)])
    for k, (dx, dy) in enumerate(PLANE):
        cols = slice(k % 4 * LANES, (k % 4 + 1) * LANES)
        rows_lse[k // 4, :, cols] = rbuf[0, pl.ds(image_slot(dx, dy), 1), :]
    for k in range(len(line)):
        recv(f"C{k}", cbuf.at[k + 1])
    cbuf[0] = lse2([cbuf[k] for k in (Z + 1, *range(1, Z))])
    for b, (dz, dc) in enumerate(texts):
        col = cbuf[0, pl.ds(text_slot(dz, dc), 1), :]
        tmax[b * LANES : (b + 1) * LANES, :] = jnp.broadcast_to(col, (LANES, LANES)).T

    for ic in (3, 2, 1, 0):
        row = rows_lse[ic]

        def second_pass(t, carry):
            acc, radial = carry
            rows = pl.ds(pl.multiple_of(t * 2 * TB, 2 * TB), 2 * TB)
            block = logit[ic, rows, :]
            col = tmax[rows, :]
            col = jnp.concatenate([col] * (IB // LANES), axis=1)
            weights = (jnp.exp2(block - row) + jnp.exp2(block - col)).astype(jnp.bfloat16)
            acc += jnp.dot(zr[t], weights, preferred_element_type=jnp.float32)
            radial += jnp.sum(
                (weights.astype(jnp.float32) * block).reshape(2 * TB // 8, 8, IB), axis=0
            )
            return acc, radial

        acc, radial = lax.fori_loop(
            0, n_t // 2, second_pass,
            (jnp.zeros((64, IB), jnp.float32), jnp.zeros((8, IB), jnp.float32)),
        )
        for q in range(4):
            k, cols = ic * 4 + q, slice(q * LANES, (q + 1) * LANES)
            msg[k, 0:64, :] = acc[:, cols]
            msg[k, 64:72, :] = radial[:, cols]
            if k > 0:
                send(f"P{k}", msg.at[k], precv.at[k - 1], dev(*PLANE[k]))

    total = msg[0]
    for k in range(len(PLANE) - 1, 0, -1):
        recv(f"P{k}", precv.at[k - 1])
        total += precv[k - 1]
    pulled = 50.0 * total[0:64] - 100.0 * own_zr
    radial = (0.5 / LOG2E) * jnp.sum(total[64:72], axis=0, keepdims=True) - own_logit
    grad = (pulled - radial * izr) / norm

    def with_features(to):
        return jnp.concatenate([grad, fbuf[pl.ds(pl.multiple_of(to * 8, 8), 8), :]], axis=0)

    for k, (dx, h) in enumerate(mates):
        to = mate(dx, h)
        gmsg[k] = with_features(to["feat"])
        send(f"g{dx}{h}", gmsg.at[k], gall.at[feat], to)
    gall[feat] = with_features(feat)
    for dx, h in mates:
        came = mate(-dx, h)["feat"]
        recv(f"m{dx}{h}", maskall.at[:, pl.ds(pl.multiple_of(came * pairs, pairs), pairs)])
    for dx, h in mates:
        recv(f"g{dx}{h}", gall.at[mate(-dx, h)["feat"]])

    shrink = 1.0 / math.sqrt(cfg["vw"])
    for f in range(2 * X):
        g = gall[f, 0:64]
        for a in range(8):
            phi[a * 64 : (a + 1) * 64, f * pairs : (f + 1) * pairs] = (
                gall[f, 64 + a : 65 + a, :] * g * shrink
            ).astype(jnp.bfloat16)
    summed = dot_nt(maskall[...], phi[...])
    high = summed.astype(jnp.bfloat16)
    rest = summed - high.astype(jnp.float32)
    mid = rest.astype(jnp.bfloat16)
    low = (rest - mid.astype(jnp.float32)).astype(jnp.bfloat16)
    tests = tg[...]
    scores = dot_nt(high, tests) + (dot_nt(mid, tests) + dot_nt(low, tests))
    tot[...] = scores.reshape(tot.shape)

    send("core", tot.at[:, :, 1 - c], crecv, dev(0, 0, 0, 1))
    recv("core", crecv)
    both = tot[:, :, c] + crecv[...]
    lane = lax.broadcasted_iota(jnp.int32, (HZ * 8, LANES), 1)
    for ylow in range(2):
        low_z = both[ylow, :HZ].reshape(HZ * 8, -1)
        high_z = both[ylow, HZ:].reshape(HZ * 8, -1)
        for xx in range(X):
            cols = slice(xx * LANES, (xx + 1) * LANES)
            a, b = low_z[:, cols], high_z[:, cols]
            first = jnp.where(lane < 64, a, pltpu.roll(b, 64, 1))
            second = jnp.where(lane < 64, pltpu.roll(a, 64, 1), b)
            pk[xx * Y + ylow] = first.reshape(HZ, 8, LANES)
            pk[xx * Y + 2 + ylow] = second.reshape(HZ, 8, LANES)
    own = image_slot(0, 0)
    for k, (dx, dy) in enumerate(plane):
        send(f"Q{k}", pk.at[image_slot(dx, dy)], prs.at[k], dev(dx, dy))
    total = pk[own]
    for k in range(len(plane)):
        recv(f"Q{k}", prs.at[k])
        total += prs[k]
    acc2[...] = total
    for dz in line:
        dz = dz % Z
        send(f"Z{dz}", acc2.at[zs[dz] & (HZ - 1)], zrs.at[dz - 1], dev(0, 0, dz, 0))
    total = acc2[z & (HZ - 1)]
    for dz in range(1, Z):
        recv(f"Z{dz}", zrs.at[dz - 1])
        total += zrs[dz - 1]
    total = jnp.where(z >= HZ, pltpu.roll(total, 64, 1), total)
    out_ref[...] = total[:, :64] * (1.0 / cfg["divide"])
    drain()


def on_device(*args):
    image_feats, text_feats, image_head, text_head, sign_image, sign_embed, tests, masks = args
    pairs, vw = image_feats.shape
    width = image_head.shape[1]
    Z = lax.axis_size("dp") // 4
    n_devices = lax.axis_size("dp") * lax.axis_size("feat")
    cfg = {"pairs": pairs, "Z": Z, "vw": vw, "divide": math.sqrt(pairs * n_devices * 4096)}
    n_image, n_text = X * Y * pairs, 2 * Z * pairs
    subsets, n_tests = masks.shape[0], tests.shape[0]
    f32, bf16 = jnp.float32, jnp.bfloat16
    vmem = pltpu.VMEM
    operands = (
        image_feats, text_feats, image_head, text_head, sign_image.T, sign_embed.T, masks, tests,
    )
    n_copies = 40 + 4 * Z - 4 + Z + 15 + Z + 15 + 14 + 1 + 15 + Z - 1
    scratch = [vmem(value.shape, value.dtype) for value in operands] + [
        vmem((64, width), bf16),
        vmem((n_image, width), bf16),
        vmem((n_text, width), bf16),
        vmem((X * Y // 4, n_text, 4 * pairs), f32),
        vmem((n_text // (4 * pairs), 64, 4 * pairs), bf16),
        vmem((n_text, LANES), f32),
        vmem((n_text, LANES), f32),
        vmem((X * Y // 4, 8, 4 * pairs), f32),
        vmem((X * Y // 4, 8, 4 * pairs), f32),
        vmem((X * Y, X * Y, pairs), f32),
        vmem((Z + 2, 2 * Z, pairs), f32),
        vmem((X * Y // 4, 1, 4 * pairs), f32),
        vmem((X * Y, 72, pairs), f32),
        vmem((X * Y - 1, 72, pairs), f32),
        vmem((64, pairs), f32),
        vmem((2 * X - 1, 72, pairs), f32),
        vmem((2 * X, 72, pairs), f32),
        vmem((subsets, 2 * X * pairs), bf16),
        vmem((512, 2 * X * pairs), bf16),
        vmem((2, Z, 2, 8, n_tests), f32),
        vmem((2, Z, 8, n_tests), f32),
        vmem((X * Y, Z // 2, 8, LANES), f32),
        vmem((X * Y - 1, Z // 2, 8, LANES), f32),
        vmem((Z // 2, 8, LANES), f32),
        vmem((Z - 1, 8, LANES), f32),
        pltpu.SemaphoreType.DMA((n_copies,)),
        pltpu.SemaphoreType.DMA((n_copies,)),
        pltpu.SemaphoreType.DMA((len(operands) + 6,)),
    ]
    return pl.pallas_call(
        functools.partial(kernel, cfg),
        out_shape=jax.ShapeDtypeStruct((8, 64), f32),
        in_specs=[pl.BlockSpec(memory_space=pl.ANY)] * len(operands),
        out_specs=pl.BlockSpec(memory_space=pltpu.VMEM),
        scratch_shapes=scratch,
        compiler_params=pltpu.CompilerParams(
            collective_id=0, has_side_effects=True, vmem_limit_bytes=60 * 1024 * 1024
        ),
    )(*operands)


def solution(mesh):
    placed = (
        P(("dp", "feat"), None),
        P(("dp", "feat"), None),
        P(),
        P(),
        P(),
        P(),
        P(None, "feat"),
        P(None, ("dp", "feat")),
    )
    return jax.shard_map(
        on_device, mesh=mesh, in_specs=placed, out_specs=P("dp", "feat"), check_vma=False
    )
```

```python
import functools
import math

import jax
import jax.numpy as jnp
from jax import lax
from jax.experimental import pallas as pl
from jax.experimental.pallas import tpu as pltpu
from jax.sharding import PartitionSpec as P

X, Y = 4, 4
LANES = 128
LOG2E = math.log2(math.e)
MESH = pl.DeviceIdType.MESH
NT = (((1,), (1,)), ((), ()))


def dot_nt(a, b):
    return lax.dot_general(a, b, NT, preferred_element_type=jnp.float32)


def lse2(parts):
    top = functools.reduce(jnp.maximum, parts)
    total = functools.reduce(lambda a, b: a + b, [jnp.exp2(p - top) for p in parts])
    return top + jnp.log2(total)


class Names:
    def __init__(self):
        self.ids = {}

    def __call__(self, name):
        return self.ids.setdefault(name, len(self.ids))


PLANE = (
    (0, 0), (1, 0), (-1, 0), (0, 1),
    (0, -1), (1, 1), (1, -1), (-1, 1),
    (-1, -1), (2, 0), (0, 2), (2, 1),
    (2, -1), (1, 2), (-1, 2), (2, 2),
)


def kernel(
    cfg,
    feats_hbm, tfeats_hbm, ihead_hbm, thead_hbm, signi_hbm, signe_hbm, mask_hbm, tg_hbm,
    out_ref,
    feats, tfeats, ihead, thead, signi, signe, masks, tg,
    sgne, img, txt, logit, zr, tmax, tsum, imax, isum, rbuf, cbuf, rows_lse, msg, precv,
    fbuf, gmsg, gall, maskall, phi, tot, csend, crecv, pk, prs, acc2, zrs,
    send_sem, recv_sem, load_sem,
):
    pairs, Z, TB = cfg["pairs"], cfg["Z"], 2 * cfg["pairs"]
    IB = 4 * pairs
    half, quarter = pairs // 2, pairs // 4
    HZ = Z // 2
    order = [0] + [d for k in range(1, HZ) for d in (k, -k)] + [HZ]
    dp, feat = lax.axis_index("dp"), lax.axis_index("feat")
    c = dp & 1
    z = (dp >> 1) & (Z - 1)
    yl = dp >> (Z.bit_length())
    x = feat >> 1
    y = ((feat & 1) << 1) + yl

    xs = [(x + d) & (X - 1) for d in range(X)]
    ys = [(y + d) & (Y - 1) for d in range(Y)]
    zs = [(z + d) & (Z - 1) for d in range(Z)]
    cs = [c, 1 - c]
    x_part = [v << 1 for v in xs]
    y_feat = [v >> 1 for v in ys]
    y_dp = [(v & 1) << (Z.bit_length()) for v in ys]
    z_part = [v << 1 for v in zs]

    def dev(dx=0, dy=0, dz=0, dc=0):
        return {
            "dp": y_dp[dy % Y] + z_part[dz % Z] + cs[dc % 2],
            "feat": x_part[dx % X] + y_feat[dy % Y],
        }

    def image_slot(dx, dy):
        return (xs[dx % X] << 2) + ys[dy % Y]

    def text_slot(dz, dc):
        return cs[dc % 2] * Z + zs[dz % Z]

    plane = PLANE[:0:-1]
    line = order[:0:-1]
    mates = [(2, 1), (1, 1), (-1, 1), (2, 0), (0, 1), (1, 0), (-1, 0)]

    def mate(dx, h):
        return {
            "dp": ((yl ^ h) << Z.bit_length()) + z_part[0] + c,
            "feat": x_part[dx % X] + (y_feat[0] ^ h),
        }

    loads = []

    def load(src, dst):
        copy = pltpu.make_async_copy(src, dst, load_sem.at[len(loads)])
        copy.start()
        loads.append(copy)
        return copy

    def load_head(src, dst):
        depth = src.shape[0]
        cuts = [0, 3 * LANES, 6 * LANES, 9 * LANES, depth]
        return [
            (load(src.at[a:b, :], dst.at[a:b, :]), a, b)
            for a, b in zip(cuts, cuts[1:])
            if a < b
        ]

    feats_load = load(feats_hbm, feats)
    ihead_loads = load_head(ihead_hbm, ihead)

    barrier = pltpu.get_barrier_semaphore()
    near = [(0, 0, 0, 1)]
    for d in (1, -1):
        near += [(d, 0, 0, 0), (0, d, 0, 0), (0, 0, d, 0)]
    for offsets in near:
        pl.semaphore_signal(barrier, inc=1, device_id=dev(*offsets), device_id_type=MESH)

    tfeats_load = load(tfeats_hbm, tfeats)
    thead_loads = load_head(thead_hbm, thead)
    other_loads = [
        load(signe_hbm, signe), load(signi_hbm, signi), load(mask_hbm, masks), load(tg_hbm, tg)
    ]

    names = Names()
    started = []

    def send(name, src, dst, to):
        i = names(name)
        copy = pltpu.make_async_remote_copy(
            src_ref=src, dst_ref=dst, send_sem=send_sem.at[i], recv_sem=recv_sem.at[i],
            device_id=to, device_id_type=MESH,
        )
        copy.start()
        started.append(copy)

    def recv(name, dst):
        i = names(name)
        pltpu.make_async_remote_copy(
            src_ref=dst, dst_ref=dst, send_sem=send_sem.at[i], recv_sem=recv_sem.at[i],
            device_id=dev(1), device_id_type=MESH,
        ).wait_recv()

    def drain():
        for copy in started:
            copy.wait_send()
        started.clear()

    def wrap(d, n):
        return (d + n // 2 - 1) % n - (n // 2 - 1)

    def image(dx, dy, r0, n):
        k = PLANE.index((wrap(dx, X), wrap(dy, Y)))
        return img.at[pl.ds(k * pairs + r0, n), :]

    def text(dz, dc, r0, n):
        k = order.index(wrap(dz, Z)) * 2 + dc % 2
        return txt.at[pl.ds(k * pairs + r0, n), :]

    def project(feats_load, feats_ref, head_loads, head_ref):
        feats_load.wait()
        proj = None
        for copy, a, b in head_loads:
            copy.wait()
            term = jnp.dot(
                feats_ref[:, a:b], head_ref[a:b, :], preferred_element_type=jnp.float32
            )
            proj = term if proj is None else proj + term
        length = jnp.sqrt(jnp.sum(proj * proj, axis=1, keepdims=True) + 1e-06)
        return (proj / length).astype(jnp.bfloat16), length

    def text_pieces(s, up):
        if s < HZ - 1:
            return (0, 1, 2, 3)
        return (0, 1) if up else (2, 3)

    def text_send(s, q):
        for up, step in ((True, 1), (False, -1)):
            if q in text_pieces(s, up):
                src = text(-s * step, 0, q * quarter, quarter)
                dst = text(-(s + 1) * step, 0, q * quarter, quarter)
                send(f"z{step}{s}{q}", src, dst, dev(0, 0, step, 0))

    def text_recv(s, q):
        for up, step in ((True, 1), (False, -1)):
            if q in text_pieces(s, up):
                recv(f"z{step}{s}{q}", text(-(s + 1) * step, 0, q * quarter, quarter))

    def text_next(s, *qs):
        for q in qs:
            text_recv(s, q)
            text_send(s + 1, q)

    def text_share(dz):
        send(f"s{dz}", text(dz, 0, 0, pairs), text(dz, 1, 0, pairs), dev(0, 0, 0, 1))

    def text_shared(dz):
        recv(f"s{dz}", text(dz, 1, 0, pairs))

    def axes(which):
        return ((1, 0), (0, 1)) if which == 0 else ((0, 1), (1, 0))

    def at(which, a, b, r0, n):
        (fx, fy), (gx, gy) = axes(which)
        return image(fx * a + gx * b, fy * a + gy * b, which * half + r0, n)

    def part(d):
        return 0 if d == 1 else quarter

    def first_send(which):
        (fx, fy), _ = axes(which)
        for d in (1, -1):
            src, dst = at(which, 0, 0, 0, half), at(which, -d, 0, 0, half)
            send(f"f{which}{d}", src, dst, dev(fx * d, fy * d))

    def first_forward(which):
        (fx, fy), _ = axes(which)
        for d in (1, -1):
            recv(f"f{which}{d}", at(which, -d, 0, 0, half))
            src = at(which, -d, 0, part(d), quarter)
            send(f"F{which}{d}", src, at(which, 2, 0, part(d), quarter), dev(fx * d, fy * d))

    def first_last(which):
        for d in (1, -1):
            recv(f"F{which}{d}", at(which, 2, 0, part(d), quarter))

    def second_send(which, a):
        _, (gx, gy) = axes(which)
        for d in (1, -1):
            src, dst = at(which, a, 0, 0, half), at(which, a, -d, 0, half)
            send(f"g{which}{a}{d}", src, dst, dev(gx * d, gy * d))

    def second_forward(which, a):
        _, (gx, gy) = axes(which)
        for d in (1, -1):
            recv(f"g{which}{a}{d}", at(which, a, -d, 0, half))
            src = at(which, a, -d, part(d), quarter)
            send(f"G{which}{a}{d}", src, at(which, a, 2, part(d), quarter), dev(gx * d, gy * d))

    def second_last(which, a):
        for d in (1, -1):
            recv(f"G{which}{a}{d}", at(which, a, 2, part(d), quarter))

    scale = 100.0 * LOG2E

    def tile(t, n, ic, h=None):
        rows = slice(t * TB, (t + n) * TB)
        width = IB if h is None else IB // 2
        c0 = 0 if h is None else h * width
        cols = slice(c0, c0 + width)
        block = dot_nt(txt[rows, :], img[ic * IB + c0 : ic * IB + c0 + width, :]) * scale
        logit[ic, rows, cols] = block
        deep = block.reshape(n * TB // 8, 8, width)
        old = imax[ic, :, cols]
        new = jnp.maximum(old, jnp.max(deep, axis=0))
        total = jnp.sum(jnp.exp2(deep - new[None]), axis=0)
        isum[ic, :, cols] = isum[ic, :, cols] * jnp.exp2(old - new) + total
        imax[ic, :, cols] = new
        parts = [block[:, k : k + LANES] for k in range(0, width, LANES)]
        old = tmax[rows, :]
        new = functools.reduce(jnp.maximum, parts, old)
        tsum[rows, :] = functools.reduce(
            lambda a, b: a + b,
            [jnp.exp2(p - new) for p in parts],
            tsum[rows, :] * jnp.exp2(old - new),
        )
        tmax[rows, :] = new

    def tiles(*steps):
        for step in steps:
            tile(*step)

    n_t = len(order)

    own_image, length = project(feats_load, feats, ihead_loads, ihead)
    img[0:pairs, :] = own_image
    pl.semaphore_wait(barrier, len(near))
    for which in (0, 1):
        first_send(which)
    for which in (0, 1):
        second_send(which, 0)
    own_text, _ = project(tfeats_load, tfeats, thead_loads, thead)
    txt[0:pairs, :] = own_text
    for q in range(4):
        text_send(0, q)
    text_share(0)

    for copy in other_loads:
        copy.wait()
    sgne[...] = (2 * signe[...] - 1).astype(jnp.bfloat16)
    norm = jnp.broadcast_to(length, (pairs, LANES)).T[0:1, :]
    izr = dot_nt(sgne[...], own_image)
    own_zr = dot_nt(sgne[...], own_text).astype(jnp.bfloat16).astype(jnp.float32)
    prod = own_image.astype(jnp.float32) * own_text.astype(jnp.float32)
    lanes = functools.reduce(
        lambda a, b: a + b, [prod[:, k : k + LANES] for k in range(0, prod.shape[1], LANES)]
    )
    own_logit = 100.0 * jnp.sum(lanes.T, axis=0, keepdims=True)
    fbuf[...] = dot_nt((2 * signi[...] - 1).astype(jnp.bfloat16), feats[...])
    mine = pl.ds(pl.multiple_of(feat * pairs, pairs), pairs)
    maskall[:, mine] = masks[...].astype(jnp.bfloat16)
    tmax[...] = jnp.full(tmax.shape, -1e30, jnp.float32)
    tsum[...] = jnp.zeros(tsum.shape, jnp.float32)
    imax[...] = jnp.full(imax.shape, -1e30, jnp.float32)
    isum[...] = jnp.zeros(isum.shape, jnp.float32)

    for which in (0, 1):
        first_forward(which)
        second_send(which, -1)
        second_send(which, 1)
    text_next(0, 0, 1)
    for which in (0, 1):
        second_forward(which, 0)
    text_next(0, 2)
    for which in (0, 1):
        first_last(which)
        second_send(which, 2)
    text_next(0, 3)
    text_share(1)
    text_share(-1)
    text_next(1, 0)
    for dz in (0, 1, -1):
        text_shared(dz)
    tiles((0, 1, 0), (1, 1, 0), (2, 1, 0))
    text_next(1, 1)
    for which in (0, 1):
        second_forward(which, -1)
    text_next(1, 2)
    for which in (0, 1):
        second_forward(which, 1)
    text_next(1, 3)
    text_share(2)
    text_share(-2)
    tiles((0, 1, 1), (1, 1, 1), (2, 1, 1))
    text_next(2, 0)
    text_shared(2)
    text_shared(-2)
    tiles((3, 1, 0), (3, 1, 1), (4, 1, 0), (4, 1, 1))
    text_next(2, 1)
    for which in (0, 1):
        second_forward(which, 2)
    for which in (0, 1):
        second_last(which, 0)
    text_next(2, 2)
    tiles((0, 2, 2, 0), (2, 3, 2, 0))
    text_next(2, 3)
    text_share(3)
    text_share(-3)
    for dx, h in mates:
        send(f"m{dx}{h}", maskall.at[:, mine], maskall.at[:, mine], mate(dx, h))
    for which in (0, 1):
        for a in (-1, 1):
            second_last(which, a)
    tiles((0, 2, 2, 1), (2, 3, 2, 1), (0, 2, 3, 0), (2, 3, 3, 0))
    for q in range(4):
        text_recv(HZ - 1, q)
    text_share(HZ)
    text_shared(3)
    text_shared(-3)
    tiles(*[(t, 1, ic) for t in (5, 6) for ic in range(3)], (5, 2, 3, 0))
    for which in (0, 1):
        second_last(which, 2)
    text_shared(HZ)
    tiles((7, 1, 0), (7, 1, 1), (7, 1, 2), (7, 1, 3))
    tiles((0, 2, 3, 1), (2, 2, 3, 1), (4, 3, 3, 1))

    texts = [(dz, dc) for dz in order for dc in range(2)]
    for b, (dz, dc) in enumerate(texts):
        rows = slice(b * LANES, (b + 1) * LANES)
        high = tmax[rows, :].T
        top = jnp.max(high, axis=0, keepdims=True)
        total = jnp.sum(tsum[rows, :].T * jnp.exp2(high - top), axis=0, keepdims=True)
        cbuf[0, pl.ds(text_slot(dz, dc), 1), :] = top + jnp.log2(total)
    send("D", cbuf.at[0], cbuf.at[Z], dev(0, 0, 0, 1))
    for k, (dx, dy) in enumerate(PLANE):
        ic, cols = k // 4, slice(k % 4 * LANES, (k % 4 + 1) * LANES)
        high = imax[ic, :, cols]
        top = jnp.max(high, axis=0, keepdims=True)
        total = jnp.sum(isum[ic, :, cols] * jnp.exp2(high - top), axis=0, keepdims=True)
        rbuf[0, pl.ds(image_slot(dx, dy), 1), :] = top + jnp.log2(total)
    for k, (dx, dy) in enumerate(plane):
        send(f"R{k}", rbuf.at[0], rbuf.at[k + 1], dev(dx, dy))
    recv("D", cbuf.at[Z])
    cbuf[Z + 1] = lse2([cbuf[0], cbuf[Z]])
    for k, dz in enumerate(line):
        send(f"C{k}", cbuf.at[Z + 1], cbuf.at[k + 1], dev(0, 0, dz, 0))

    for t in range(n_t // 2):
        rows = slice(t * 2 * TB, (t + 1) * 2 * TB)
        zr[t] = dot_nt(sgne[...], txt[rows, :]).astype(jnp.bfloat16)
    drain()

    for k in range(len(plane)):
        recv(f"R{k}", rbuf.at[k + 1])
    rbuf[0] = lse2([rbuf[k] for k in range(len(plane) + 1)])
    for k, (dx, dy) in enumerate(PLANE):
        cols = slice(k % 4 * LANES, (k % 4 + 1) * LANES)
        rows_lse[k // 4, :, cols] = rbuf[0, pl.ds(image_slot(dx, dy), 1), :]
    for k in range(len(line)):
        recv(f"C{k}", cbuf.at[k + 1])
    cbuf[0] = lse2([cbuf[k] for k in (Z + 1, *range(1, Z))])
    for b, (dz, dc) in enumerate(texts):
        col = cbuf[0, pl.ds(text_slot(dz, dc), 1), :]
        tmax[b * LANES : (b + 1) * LANES, :] = jnp.broadcast_to(col, (LANES, LANES)).T

    for ic in (3, 2, 1, 0):
        row = rows_lse[ic]

        def second_pass(t, carry):
            acc, radial = carry
            rows = pl.ds(pl.multiple_of(t * 2 * TB, 2 * TB), 2 * TB)
            block = logit[ic, rows, :]
            col = tmax[rows, :]
            col = jnp.concatenate([col] * (IB // LANES), axis=1)
            weights = (jnp.exp2(block - row) + jnp.exp2(block - col)).astype(jnp.bfloat16)
            acc += jnp.dot(zr[t], weights, preferred_element_type=jnp.float32)
            radial += jnp.sum(
                (weights.astype(jnp.float32) * block).reshape(2 * TB // 8, 8, IB), axis=0
            )
            return acc, radial

        acc, radial = lax.fori_loop(
            0, n_t // 2, second_pass,
            (jnp.zeros((64, IB), jnp.float32), jnp.zeros((8, IB), jnp.float32)),
        )
        for q in range(4):
            k, cols = ic * 4 + q, slice(q * LANES, (q + 1) * LANES)
            msg[k, 0:64, :] = acc[:, cols]
            msg[k, 64:72, :] = radial[:, cols]
            if k > 0:
                send(f"P{k}", msg.at[k], precv.at[k - 1], dev(*PLANE[k]))

    total = msg[0]
    for k in range(len(PLANE) - 1, 0, -1):
        recv(f"P{k}", precv.at[k - 1])
        total += precv[k - 1]
    pulled = 50.0 * total[0:64] - 100.0 * own_zr
    radial = (0.5 / LOG2E) * jnp.sum(total[64:72], axis=0, keepdims=True) - own_logit
    grad = (pulled - radial * izr) / norm

    def with_features(to):
        return jnp.concatenate([grad, fbuf[pl.ds(pl.multiple_of(to * 8, 8), 8), :]], axis=0)

    for k, (dx, h) in enumerate(mates):
        to = mate(dx, h)
        gmsg[k] = with_features(to["feat"])
        send(f"g{dx}{h}", gmsg.at[k], gall.at[feat], to)
    gall[feat] = with_features(feat)
    for dx, h in mates:
        came = mate(-dx, h)["feat"]
        recv(f"m{dx}{h}", maskall.at[:, pl.ds(pl.multiple_of(came * pairs, pairs), pairs)])
    for dx, h in mates:
        recv(f"g{dx}{h}", gall.at[mate(-dx, h)["feat"]])

    shrink = 1.0 / math.sqrt(cfg["vw"])
    for f in range(2 * X):
        g = gall[f, 0:64]
        for a in range(8):
            phi[a * 64 : (a + 1) * 64, f * pairs : (f + 1) * pairs] = (
                gall[f, 64 + a : 65 + a, :] * g * shrink
            ).astype(jnp.bfloat16)
    summed = dot_nt(maskall[...], phi[...])
    tot[...] = summed.reshape(tot.shape)
    tests = tg[...]

    def score(part):
        high = part.astype(jnp.bfloat16)
        rest = part - high.astype(jnp.float32)
        mid = rest.astype(jnp.bfloat16)
        low = (rest - mid.astype(jnp.float32)).astype(jnp.bfloat16)
        return dot_nt(high, tests) + (dot_nt(mid, tests) + dot_nt(low, tests))

    n_rows = 2 * Z * 8
    theirs = score(tot[:, :, 1 - c].reshape(n_rows, -1))
    csend[...] = theirs.reshape(csend.shape)
    send("core", csend, crecv, dev(0, 0, 0, 1))
    both = score(tot[:, :, c].reshape(n_rows, -1)).reshape(csend.shape)
    recv("core", crecv)
    both = both + crecv[...]
    lane = lax.broadcasted_iota(jnp.int32, (HZ * 8, LANES), 1)
    for ylow in range(2):
        low_z = both[ylow, :HZ].reshape(HZ * 8, -1)
        high_z = both[ylow, HZ:].reshape(HZ * 8, -1)
        for xx in range(X):
            cols = slice(xx * LANES, (xx + 1) * LANES)
            a, b = low_z[:, cols], high_z[:, cols]
            first = jnp.where(lane < 64, a, pltpu.roll(b, 64, 1))
            second = jnp.where(lane < 64, pltpu.roll(a, 64, 1), b)
            pk[xx * Y + ylow] = first.reshape(HZ, 8, LANES)
            pk[xx * Y + 2 + ylow] = second.reshape(HZ, 8, LANES)
    own = image_slot(0, 0)
    for k, (dx, dy) in enumerate(plane):
        send(f"Q{k}", pk.at[image_slot(dx, dy)], prs.at[k], dev(dx, dy))
    total = pk[own]
    for k in range(len(plane)):
        recv(f"Q{k}", prs.at[k])
        total += prs[k]
    acc2[...] = total
    for dz in line:
        dz = dz % Z
        send(f"Z{dz}", acc2.at[zs[dz] & (HZ - 1)], zrs.at[dz - 1], dev(0, 0, dz, 0))
    total = acc2[z & (HZ - 1)]
    for dz in range(1, Z):
        recv(f"Z{dz}", zrs.at[dz - 1])
        total += zrs[dz - 1]
    total = jnp.where(z >= HZ, pltpu.roll(total, 64, 1), total)
    out_ref[...] = total[:, :64] * (1.0 / cfg["divide"])
    drain()


def on_device(*args):
    image_feats, text_feats, image_head, text_head, sign_image, sign_embed, tests, masks = args
    pairs, vw = image_feats.shape
    width = image_head.shape[1]
    Z = lax.axis_size("dp") // 4
    n_devices = lax.axis_size("dp") * lax.axis_size("feat")
    cfg = {"pairs": pairs, "Z": Z, "vw": vw, "divide": math.sqrt(pairs * n_devices * 4096)}
    n_image, n_text = X * Y * pairs, 2 * Z * pairs
    subsets, n_tests = masks.shape[0], tests.shape[0]
    f32, bf16 = jnp.float32, jnp.bfloat16
    vmem = pltpu.VMEM
    operands = (
        image_feats, text_feats, image_head, text_head, sign_image.T, sign_embed.T, masks, tests,
    )
    n_copies = 40 + 4 * Z - 4 + Z + 15 + Z + 15 + 14 + 1 + 15 + Z - 1
    scratch = [vmem(value.shape, value.dtype) for value in operands] + [
        vmem((64, width), bf16),
        vmem((n_image, width), bf16),
        vmem((n_text, width), bf16),
        vmem((X * Y // 4, n_text, 4 * pairs), f32),
        vmem((n_text // (4 * pairs), 64, 4 * pairs), bf16),
        vmem((n_text, LANES), f32),
        vmem((n_text, LANES), f32),
        vmem((X * Y // 4, 8, 4 * pairs), f32),
        vmem((X * Y // 4, 8, 4 * pairs), f32),
        vmem((X * Y, X * Y, pairs), f32),
        vmem((Z + 2, 2 * Z, pairs), f32),
        vmem((X * Y // 4, 1, 4 * pairs), f32),
        vmem((X * Y, 72, pairs), f32),
        vmem((X * Y - 1, 72, pairs), f32),
        vmem((64, pairs), f32),
        vmem((2 * X - 1, 72, pairs), f32),
        vmem((2 * X, 72, pairs), f32),
        vmem((subsets, 2 * X * pairs), bf16),
        vmem((512, 2 * X * pairs), bf16),
        vmem((2, Z, 2, 8, 512), f32),
        vmem((2, Z, 8, n_tests), f32),
        vmem((2, Z, 8, n_tests), f32),
        vmem((X * Y, Z // 2, 8, LANES), f32),
        vmem((X * Y - 1, Z // 2, 8, LANES), f32),
        vmem((Z // 2, 8, LANES), f32),
        vmem((Z - 1, 8, LANES), f32),
        pltpu.SemaphoreType.DMA((n_copies,)),
        pltpu.SemaphoreType.DMA((n_copies,)),
        pltpu.SemaphoreType.DMA((len(operands) + 6,)),
    ]
    return pl.pallas_call(
        functools.partial(kernel, cfg),
        out_shape=jax.ShapeDtypeStruct((8, 64), f32),
        in_specs=[pl.BlockSpec(memory_space=pl.ANY)] * len(operands),
        out_specs=pl.BlockSpec(memory_space=pltpu.VMEM),
        scratch_shapes=scratch,
        compiler_params=pltpu.CompilerParams(
            collective_id=0, has_side_effects=True, vmem_limit_bytes=60 * 1024 * 1024
        ),
    )(*operands)


def solution(mesh):
    placed = (
        P(("dp", "feat"), None),
        P(("dp", "feat"), None),
        P(),
        P(),
        P(),
        P(),
        P(None, "feat"),
        P(None, ("dp", "feat")),
    )
    return jax.shard_map(
        on_device, mesh=mesh, in_specs=placed, out_specs=P("dp", "feat"), check_vma=False
    )
```

```python
import functools
import math

import jax
import jax.numpy as jnp
from jax import lax
from jax.experimental import pallas as pl
from jax.experimental.pallas import tpu as pltpu
from jax.sharding import PartitionSpec as P

X, Y = 4, 4
LANES = 128
LOG2E = math.log2(math.e)
MESH = pl.DeviceIdType.MESH
NT = (((1,), (1,)), ((), ()))


def dot_nt(a, b):
    return lax.dot_general(a, b, NT, preferred_element_type=jnp.float32)


def lse2(parts):
    top = functools.reduce(jnp.maximum, parts)
    total = functools.reduce(lambda a, b: a + b, [jnp.exp2(p - top) for p in parts])
    return top + jnp.log2(total)


class Names:
    def __init__(self):
        self.ids = {}

    def __call__(self, name):
        return self.ids.setdefault(name, len(self.ids))


PLANE = (
    (0, 0), (1, 0), (-1, 0), (0, 1),
    (0, -1), (1, 1), (1, -1), (-1, 1),
    (-1, -1), (2, 0), (0, 2), (2, 1),
    (2, -1), (1, 2), (-1, 2), (2, 2),
)


def kernel(
    cfg,
    feats_hbm, tfeats_hbm, ihead_hbm, thead_hbm, signi_hbm, signe_hbm, mask_hbm, tg_hbm,
    out_ref,
    feats, tfeats, ihead, thead, signi, signe, masks, tg,
    sgne, img, txt, logit, zr, tmax, tsum, imax, isum, rbuf, cbuf, rows_lse, msg, precv,
    fbuf, gmsg, gall, maskall, phi, tot, crecv, pk, prs, acc2, zrs,
    send_sem, recv_sem, load_sem,
):
    pairs, Z, TB = cfg["pairs"], cfg["Z"], 2 * cfg["pairs"]
    IB = 4 * pairs
    half, quarter = pairs // 2, pairs // 4
    HZ = Z // 2
    order = [0] + [d for k in range(1, HZ) for d in (k, -k)] + [HZ]
    dp, feat = lax.axis_index("dp"), lax.axis_index("feat")
    c = dp & 1
    z = (dp >> 1) & (Z - 1)
    yl = dp >> (Z.bit_length())
    x = feat >> 1
    y = ((feat & 1) << 1) + yl

    xs = [(x + d) & (X - 1) for d in range(X)]
    ys = [(y + d) & (Y - 1) for d in range(Y)]
    zs = [(z + d) & (Z - 1) for d in range(Z)]
    cs = [c, 1 - c]
    x_part = [v << 1 for v in xs]
    y_feat = [v >> 1 for v in ys]
    y_dp = [(v & 1) << (Z.bit_length()) for v in ys]
    z_part = [v << 1 for v in zs]

    def dev(dx=0, dy=0, dz=0, dc=0):
        return {
            "dp": y_dp[dy % Y] + z_part[dz % Z] + cs[dc % 2],
            "feat": x_part[dx % X] + y_feat[dy % Y],
        }

    def image_slot(dx, dy):
        return (xs[dx % X] << 2) + ys[dy % Y]

    def text_slot(dz, dc):
        return cs[dc % 2] * Z + zs[dz % Z]

    plane = PLANE[:0:-1]
    line = order[:0:-1]
    mates = [(2, 1), (1, 1), (-1, 1), (2, 0), (0, 1), (1, 0), (-1, 0)]

    def mate(dx, h):
        return {
            "dp": ((yl ^ h) << Z.bit_length()) + z_part[0] + c,
            "feat": x_part[dx % X] + (y_feat[0] ^ h),
        }

    loads = []

    def load(src, dst):
        copy = pltpu.make_async_copy(src, dst, load_sem.at[len(loads)])
        copy.start()
        loads.append(copy)
        return copy

    def load_head(src, dst):
        depth = src.shape[0]
        cuts = [0, 3 * LANES, 6 * LANES, 9 * LANES, depth]
        return [
            (load(src.at[a:b, :], dst.at[a:b, :]), a, b)
            for a, b in zip(cuts, cuts[1:])
            if a < b
        ]

    feats_load = load(feats_hbm, feats)
    ihead_loads = load_head(ihead_hbm, ihead)

    barrier = pltpu.get_barrier_semaphore()
    near = [(0, 0, 0, 1)]
    for d in (1, -1):
        near += [(d, 0, 0, 0), (0, d, 0, 0), (0, 0, d, 0)]
    for offsets in near:
        pl.semaphore_signal(barrier, inc=1, device_id=dev(*offsets), device_id_type=MESH)

    tfeats_load = load(tfeats_hbm, tfeats)
    thead_loads = load_head(thead_hbm, thead)
    other_loads = [
        load(signe_hbm, signe), load(signi_hbm, signi), load(mask_hbm, masks), load(tg_hbm, tg)
    ]

    names = Names()
    started = []

    def send(name, src, dst, to):
        i = names(name)
        copy = pltpu.make_async_remote_copy(
            src_ref=src, dst_ref=dst, send_sem=send_sem.at[i], recv_sem=recv_sem.at[i],
            device_id=to, device_id_type=MESH,
        )
        copy.start()
        started.append(copy)

    def recv(name, dst):
        i = names(name)
        pltpu.make_async_remote_copy(
            src_ref=dst, dst_ref=dst, send_sem=send_sem.at[i], recv_sem=recv_sem.at[i],
            device_id=dev(1), device_id_type=MESH,
        ).wait_recv()

    def drain():
        for copy in started:
            copy.wait_send()
        started.clear()

    def wrap(d, n):
        return (d + n // 2 - 1) % n - (n // 2 - 1)

    def image(dx, dy, r0, n):
        k = PLANE.index((wrap(dx, X), wrap(dy, Y)))
        return img.at[pl.ds(k * pairs + r0, n), :]

    def text(dz, dc, r0, n):
        k = order.index(wrap(dz, Z)) * 2 + dc % 2
        return txt.at[pl.ds(k * pairs + r0, n), :]

    def project(feats_load, feats_ref, head_loads, head_ref):
        feats_load.wait()
        proj = None
        for copy, a, b in head_loads:
            copy.wait()
            term = jnp.dot(
                feats_ref[:, a:b], head_ref[a:b, :], preferred_element_type=jnp.float32
            )
            proj = term if proj is None else proj + term
        length = jnp.sqrt(jnp.sum(proj * proj, axis=1, keepdims=True) + 1e-06)
        return (proj / length).astype(jnp.bfloat16), length

    def text_pieces(s, up):
        if s < HZ - 1:
            return (0, 1, 2, 3)
        return (0, 1) if up else (2, 3)

    def text_send(s, q):
        for up, step in ((True, 1), (False, -1)):
            if q in text_pieces(s, up):
                src = text(-s * step, 0, q * quarter, quarter)
                dst = text(-(s + 1) * step, 0, q * quarter, quarter)
                send(f"z{step}{s}{q}", src, dst, dev(0, 0, step, 0))

    def text_recv(s, q):
        for up, step in ((True, 1), (False, -1)):
            if q in text_pieces(s, up):
                recv(f"z{step}{s}{q}", text(-(s + 1) * step, 0, q * quarter, quarter))

    def text_next(s, *qs):
        for q in qs:
            text_recv(s, q)
            text_send(s + 1, q)

    def text_share(dz):
        send(f"s{dz}", text(dz, 0, 0, pairs), text(dz, 1, 0, pairs), dev(0, 0, 0, 1))

    def text_shared(dz):
        recv(f"s{dz}", text(dz, 1, 0, pairs))

    def axes(which):
        return ((1, 0), (0, 1)) if which == 0 else ((0, 1), (1, 0))

    def at(which, a, b, r0, n):
        (fx, fy), (gx, gy) = axes(which)
        return image(fx * a + gx * b, fy * a + gy * b, which * half + r0, n)

    def part(d):
        return 0 if d == 1 else quarter

    def first_send(which):
        (fx, fy), _ = axes(which)
        for d in (1, -1):
            src, dst = at(which, 0, 0, 0, half), at(which, -d, 0, 0, half)
            send(f"f{which}{d}", src, dst, dev(fx * d, fy * d))

    def first_forward(which):
        (fx, fy), _ = axes(which)
        for d in (1, -1):
            recv(f"f{which}{d}", at(which, -d, 0, 0, half))
            src = at(which, -d, 0, part(d), quarter)
            send(f"F{which}{d}", src, at(which, 2, 0, part(d), quarter), dev(fx * d, fy * d))

    def first_last(which):
        for d in (1, -1):
            recv(f"F{which}{d}", at(which, 2, 0, part(d), quarter))

    def second_send(which, a):
        _, (gx, gy) = axes(which)
        for d in (1, -1):
            src, dst = at(which, a, 0, 0, half), at(which, a, -d, 0, half)
            send(f"g{which}{a}{d}", src, dst, dev(gx * d, gy * d))

    def second_forward(which, a):
        _, (gx, gy) = axes(which)
        for d in (1, -1):
            recv(f"g{which}{a}{d}", at(which, a, -d, 0, half))
            src = at(which, a, -d, part(d), quarter)
            send(f"G{which}{a}{d}", src, at(which, a, 2, part(d), quarter), dev(gx * d, gy * d))

    def second_last(which, a):
        for d in (1, -1):
            recv(f"G{which}{a}{d}", at(which, a, 2, part(d), quarter))

    scale = 100.0 * LOG2E

    def tile(t, n, ic, h=None):
        rows = slice(t * TB, (t + n) * TB)
        width = IB if h is None else IB // 2
        c0 = 0 if h is None else h * width
        cols = slice(c0, c0 + width)
        block = dot_nt(txt[rows, :], img[ic * IB + c0 : ic * IB + c0 + width, :]) * scale
        logit[ic, rows, cols] = block
        deep = block.reshape(n * TB // 8, 8, width)
        old = imax[ic, :, cols]
        new = jnp.maximum(old, jnp.max(deep, axis=0))
        total = jnp.sum(jnp.exp2(deep - new[None]), axis=0)
        isum[ic, :, cols] = isum[ic, :, cols] * jnp.exp2(old - new) + total
        imax[ic, :, cols] = new
        parts = [block[:, k : k + LANES] for k in range(0, width, LANES)]
        old = tmax[rows, :]
        new = functools.reduce(jnp.maximum, parts, old)
        tsum[rows, :] = functools.reduce(
            lambda a, b: a + b,
            [jnp.exp2(p - new) for p in parts],
            tsum[rows, :] * jnp.exp2(old - new),
        )
        tmax[rows, :] = new

    def tiles(*steps):
        for step in steps:
            tile(*step)

    n_t = len(order)

    own_image, length = project(feats_load, feats, ihead_loads, ihead)
    img[0:pairs, :] = own_image
    pl.semaphore_wait(barrier, len(near))
    for which in (0, 1):
        first_send(which)
    for which in (0, 1):
        second_send(which, 0)
    own_text, _ = project(tfeats_load, tfeats, thead_loads, thead)
    txt[0:pairs, :] = own_text
    for q in range(4):
        text_send(0, q)
    text_share(0)

    for copy in other_loads:
        copy.wait()
    sgne[...] = (2 * signe[...] - 1).astype(jnp.bfloat16)
    norm = jnp.broadcast_to(length, (pairs, LANES)).T[0:1, :]
    izr = dot_nt(sgne[...], own_image)
    own_zr = dot_nt(sgne[...], own_text).astype(jnp.bfloat16).astype(jnp.float32)
    prod = own_image.astype(jnp.float32) * own_text.astype(jnp.float32)
    lanes = functools.reduce(
        lambda a, b: a + b, [prod[:, k : k + LANES] for k in range(0, prod.shape[1], LANES)]
    )
    own_logit = 100.0 * jnp.sum(lanes.T, axis=0, keepdims=True)
    fbuf[...] = dot_nt((2 * signi[...] - 1).astype(jnp.bfloat16), feats[...])
    mine = pl.ds(pl.multiple_of(feat * pairs, pairs), pairs)
    maskall[:, mine] = masks[...].astype(jnp.bfloat16)
    tmax[...] = jnp.full(tmax.shape, -1e30, jnp.float32)
    tsum[...] = jnp.zeros(tsum.shape, jnp.float32)
    imax[...] = jnp.full(imax.shape, -1e30, jnp.float32)
    isum[...] = jnp.zeros(isum.shape, jnp.float32)

    for which in (0, 1):
        first_forward(which)
        second_send(which, -1)
        second_send(which, 1)
    text_next(0, 0, 1)
    for which in (0, 1):
        second_forward(which, 0)
    text_next(0, 2)
    for which in (0, 1):
        first_last(which)
        second_send(which, 2)
    text_next(0, 3)
    text_share(1)
    text_share(-1)
    text_next(1, 0)
    for dz in (0, 1, -1):
        text_shared(dz)
    tiles((0, 1, 0), (1, 1, 0), (2, 1, 0))
    text_next(1, 1)
    for which in (0, 1):
        second_forward(which, -1)
    text_next(1, 2)
    for which in (0, 1):
        second_forward(which, 1)
    text_next(1, 3)
    text_share(2)
    text_share(-2)
    tiles((0, 1, 1), (1, 1, 1), (2, 1, 1))
    text_next(2, 0)
    text_shared(2)
    text_shared(-2)
    tiles((3, 1, 0), (3, 1, 1), (4, 1, 0), (4, 1, 1))
    text_next(2, 1)
    for which in (0, 1):
        second_forward(which, 2)
    for which in (0, 1):
        second_last(which, 0)
    text_next(2, 2)
    tiles((0, 2, 2, 0), (2, 3, 2, 0))
    text_next(2, 3)
    text_share(3)
    text_share(-3)
    for dx, h in mates:
        send(f"m{dx}{h}", maskall.at[:, mine], maskall.at[:, mine], mate(dx, h))
    for which in (0, 1):
        for a in (-1, 1):
            second_last(which, a)
    tiles((0, 2, 2, 1), (2, 3, 2, 1), (0, 2, 3, 0), (2, 3, 3, 0))
    for q in range(4):
        text_recv(HZ - 1, q)
    text_share(HZ)
    text_shared(3)
    text_shared(-3)
    tiles(*[(t, 1, ic) for t in (5, 6) for ic in range(3)], (5, 2, 3, 0))
    for which in (0, 1):
        second_last(which, 2)
    text_shared(HZ)
    tiles((7, 1, 0), (7, 1, 1), (7, 1, 2), (7, 1, 3))
    tiles((0, 2, 3, 1), (2, 2, 3, 1), (4, 3, 3, 1))

    for k, (dx, dy) in enumerate(PLANE):
        ic, cols = k // 4, slice(k % 4 * LANES, (k % 4 + 1) * LANES)
        high = imax[ic, :, cols]
        top = jnp.max(high, axis=0, keepdims=True)
        total = jnp.sum(isum[ic, :, cols] * jnp.exp2(high - top), axis=0, keepdims=True)
        rbuf[0, pl.ds(image_slot(dx, dy), 1), :] = top + jnp.log2(total)
    for k, (dx, dy) in enumerate(plane):
        send(f"R{k}", rbuf.at[0], rbuf.at[k + 1], dev(dx, dy))
    texts = [(dz, dc) for dz in order for dc in range(2)]
    for b, (dz, dc) in enumerate(texts):
        rows = slice(b * LANES, (b + 1) * LANES)
        high = tmax[rows, :].T
        top = jnp.max(high, axis=0, keepdims=True)
        total = jnp.sum(tsum[rows, :].T * jnp.exp2(high - top), axis=0, keepdims=True)
        cbuf[0, pl.ds(text_slot(dz, dc), 1), :] = top + jnp.log2(total)
    send("D", cbuf.at[0], cbuf.at[Z], dev(0, 0, 0, 1))
    recv("D", cbuf.at[Z])
    cbuf[Z + 1] = lse2([cbuf[0], cbuf[Z]])
    for k, dz in enumerate(line):
        send(f"C{k}", cbuf.at[Z + 1], cbuf.at[k + 1], dev(0, 0, dz, 0))

    for t in range(n_t // 2):
        rows = slice(t * 2 * TB, (t + 1) * 2 * TB)
        zr[t] = dot_nt(sgne[...], txt[rows, :]).astype(jnp.bfloat16)
    drain()

    for k in range(len(plane)):
        recv(f"R{k}", rbuf.at[k + 1])
    rbuf[0] = lse2([rbuf[k] for k in range(len(plane) + 1)])
    for k, (dx, dy) in enumerate(PLANE):
        cols = slice(k % 4 * LANES, (k % 4 + 1) * LANES)
        rows_lse[k // 4, :, cols] = rbuf[0, pl.ds(image_slot(dx, dy), 1), :]
    for k in range(len(line)):
        recv(f"C{k}", cbuf.at[k + 1])
    cbuf[0] = lse2([cbuf[k] for k in (Z + 1, *range(1, Z))])
    for b, (dz, dc) in enumerate(texts):
        col = cbuf[0, pl.ds(text_slot(dz, dc), 1), :]
        tmax[b * LANES : (b + 1) * LANES, :] = jnp.broadcast_to(col, (LANES, LANES)).T

    for ic in (3, 2, 1, 0):
        row = rows_lse[ic]

        def second_pass(t, carry):
            acc, radial = carry
            rows = pl.ds(pl.multiple_of(t * 2 * TB, 2 * TB), 2 * TB)
            block = logit[ic, rows, :]
            col = tmax[rows, :]
            col = jnp.concatenate([col] * (IB // LANES), axis=1)
            weights = (jnp.exp2(block - row) + jnp.exp2(block - col)).astype(jnp.bfloat16)
            acc += jnp.dot(zr[t], weights, preferred_element_type=jnp.float32)
            radial += jnp.sum(
                (weights.astype(jnp.float32) * block).reshape(2 * TB // 8, 8, IB), axis=0
            )
            return acc, radial

        acc, radial = lax.fori_loop(
            0, n_t // 2, second_pass,
            (jnp.zeros((64, IB), jnp.float32), jnp.zeros((8, IB), jnp.float32)),
            unroll=True,
        )
        for q in range(4):
            k, cols = ic * 4 + q, slice(q * LANES, (q + 1) * LANES)
            msg[k, 0:64, :] = acc[:, cols]
            msg[k, 64:72, :] = radial[:, cols]
            if k > 0:
                send(f"P{k}", msg.at[k], precv.at[k - 1], dev(*PLANE[k]))

    total = msg[0]
    for k in range(len(PLANE) - 1, 0, -1):
        recv(f"P{k}", precv.at[k - 1])
        total += precv[k - 1]
    pulled = 50.0 * total[0:64] - 100.0 * own_zr
    radial = (0.5 / LOG2E) * jnp.sum(total[64:72], axis=0, keepdims=True) - own_logit
    grad = (pulled - radial * izr) / norm

    def with_features(to):
        return jnp.concatenate([grad, fbuf[pl.ds(pl.multiple_of(to * 8, 8), 8), :]], axis=0)

    for k, (dx, h) in enumerate(mates):
        to = mate(dx, h)
        gmsg[k] = with_features(to["feat"])
        send(f"g{dx}{h}", gmsg.at[k], gall.at[feat], to)
    gall[feat] = with_features(feat)
    for dx, h in mates:
        came = mate(-dx, h)["feat"]
        recv(f"m{dx}{h}", maskall.at[:, pl.ds(pl.multiple_of(came * pairs, pairs), pairs)])
    for dx, h in mates:
        recv(f"g{dx}{h}", gall.at[mate(-dx, h)["feat"]])

    shrink = 1.0 / math.sqrt(cfg["vw"])
    for f in range(2 * X):
        g = gall[f, 0:64]
        for a in range(8):
            phi[a * 64 : (a + 1) * 64, f * pairs : (f + 1) * pairs] = (
                gall[f, 64 + a : 65 + a, :] * g * shrink
            ).astype(jnp.bfloat16)
    summed = dot_nt(maskall[...], phi[...])
    high = summed.astype(jnp.bfloat16)
    rest = summed - high.astype(jnp.float32)
    mid = rest.astype(jnp.bfloat16)
    low = (rest - mid.astype(jnp.float32)).astype(jnp.bfloat16)
    tests = tg[...]
    scores = dot_nt(high, tests) + (dot_nt(mid, tests) + dot_nt(low, tests))
    tot[...] = scores.reshape(tot.shape)

    send("core", tot.at[:, :, 1 - c], crecv, dev(0, 0, 0, 1))
    recv("core", crecv)
    both = tot[:, :, c] + crecv[...]
    lane = lax.broadcasted_iota(jnp.int32, (HZ * 8, LANES), 1)
    for ylow in range(2):
        low_z = both[ylow, :HZ].reshape(HZ * 8, -1)
        high_z = both[ylow, HZ:].reshape(HZ * 8, -1)
        for xx in range(X):
            cols = slice(xx * LANES, (xx + 1) * LANES)
            a, b = low_z[:, cols], high_z[:, cols]
            first = jnp.where(lane < 64, a, pltpu.roll(b, 64, 1))
            second = jnp.where(lane < 64, pltpu.roll(a, 64, 1), b)
            pk[xx * Y + ylow] = first.reshape(HZ, 8, LANES)
            pk[xx * Y + 2 + ylow] = second.reshape(HZ, 8, LANES)
    own = image_slot(0, 0)
    for k, (dx, dy) in enumerate(plane):
        send(f"Q{k}", pk.at[image_slot(dx, dy)], prs.at[k], dev(dx, dy))
    total = pk[own]
    for k in range(len(plane)):
        recv(f"Q{k}", prs.at[k])
        total += prs[k]
    acc2[...] = total
    for dz in line:
        dz = dz % Z
        send(f"Z{dz}", acc2.at[zs[dz] & (HZ - 1)], zrs.at[dz - 1], dev(0, 0, dz, 0))
    total = acc2[z & (HZ - 1)]
    for dz in range(1, Z):
        recv(f"Z{dz}", zrs.at[dz - 1])
        total += zrs[dz - 1]
    total = jnp.where(z >= HZ, pltpu.roll(total, 64, 1), total)
    out_ref[...] = total[:, :64] * (1.0 / cfg["divide"])
    drain()


def on_device(*args):
    image_feats, text_feats, image_head, text_head, sign_image, sign_embed, tests, masks = args
    pairs, vw = image_feats.shape
    width = image_head.shape[1]
    Z = lax.axis_size("dp") // 4
    n_devices = lax.axis_size("dp") * lax.axis_size("feat")
    cfg = {"pairs": pairs, "Z": Z, "vw": vw, "divide": math.sqrt(pairs * n_devices * 4096)}
    n_image, n_text = X * Y * pairs, 2 * Z * pairs
    subsets, n_tests = masks.shape[0], tests.shape[0]
    f32, bf16 = jnp.float32, jnp.bfloat16
    vmem = pltpu.VMEM
    operands = (
        image_feats, text_feats, image_head, text_head, sign_image.T, sign_embed.T, masks, tests,
    )
    n_copies = 40 + 4 * Z - 4 + Z + 15 + Z + 15 + 14 + 1 + 15 + Z - 1
    scratch = [vmem(value.shape, value.dtype) for value in operands] + [
        vmem((64, width), bf16),
        vmem((n_image, width), bf16),
        vmem((n_text, width), bf16),
        vmem((X * Y // 4, n_text, 4 * pairs), f32),
        vmem((n_text // (4 * pairs), 64, 4 * pairs), bf16),
        vmem((n_text, LANES), f32),
        vmem((n_text, LANES), f32),
        vmem((X * Y // 4, 8, 4 * pairs), f32),
        vmem((X * Y // 4, 8, 4 * pairs), f32),
        vmem((X * Y, X * Y, pairs), f32),
        vmem((Z + 2, 2 * Z, pairs), f32),
        vmem((X * Y // 4, 1, 4 * pairs), f32),
        vmem((X * Y, 72, pairs), f32),
        vmem((X * Y - 1, 72, pairs), f32),
        vmem((64, pairs), f32),
        vmem((2 * X - 1, 72, pairs), f32),
        vmem((2 * X, 72, pairs), f32),
        vmem((subsets, 2 * X * pairs), bf16),
        vmem((512, 2 * X * pairs), bf16),
        vmem((2, Z, 2, 8, n_tests), f32),
        vmem((2, Z, 8, n_tests), f32),
        vmem((X * Y, Z // 2, 8, LANES), f32),
        vmem((X * Y - 1, Z // 2, 8, LANES), f32),
        vmem((Z // 2, 8, LANES), f32),
        vmem((Z - 1, 8, LANES), f32),
        pltpu.SemaphoreType.DMA((n_copies,)),
        pltpu.SemaphoreType.DMA((n_copies,)),
        pltpu.SemaphoreType.DMA((len(operands) + 6,)),
    ]
    return pl.pallas_call(
        functools.partial(kernel, cfg),
        out_shape=jax.ShapeDtypeStruct((8, 64), f32),
        in_specs=[pl.BlockSpec(memory_space=pl.ANY)] * len(operands),
        out_specs=pl.BlockSpec(memory_space=pltpu.VMEM),
        scratch_shapes=scratch,
        compiler_params=pltpu.CompilerParams(
            collective_id=0, has_side_effects=True, vmem_limit_bytes=60 * 1024 * 1024
        ),
    )(*operands)


def solution(mesh):
    placed = (
        P(("dp", "feat"), None),
        P(("dp", "feat"), None),
        P(),
        P(),
        P(),
        P(),
        P(None, "feat"),
        P(None, ("dp", "feat")),
    )
    return jax.shard_map(
        on_device, mesh=mesh, in_specs=placed, out_specs=P("dp", "feat"), check_vma=False
    )
```
